128 devices in a mesh: rep: 2 (over z_hi), row: 2 (over z_lo), col: 32 (over y, x, core).
Axes of the slice: x: 4, y: 4, z: 4 (z_hi: 2, z_lo: 2; z = z_hi * 2 + z_lo), core: 2. Of those that a mesh axis runs over, the one named last changes fastest.
Arguments:
- tokens: bfloat16 [2, 32, 512, 1024], P('rep', 'row', 'col'), may hold values from -6 to 6
- cotangent: bfloat16 [2, 32, 512, 1024], P('rep', 'row', 'col'), may hold values from -6 to 6
- row_field: int32 [2, 32], P('rep'), may hold values from 0 to 8, never falling along the last dimension, each value on 1 to 16 neighbouring positions
- col_field: int32 [2, 512], P('rep'), may hold values from 0 to 63, never falling along the last dimension, each value on 1 to 16 neighbouring positions
- qkv_weight: bfloat16 [1024, 3072], replicated, may hold values from -0.1875 to 0.1875
- qkv_bias: float32 [3072], replicated, may hold values from -3 to 3
- logit_scale: float32 [32], replicated, may hold values from 2 to 20
- position_bias: float32 [32, 64, 64], replicated, may hold values from 0 to 6
- proj_weight: bfloat16 [1024, 1024], replicated, may hold values from -0.1875 to 0.1875
- proj_bias: float32 [1024], replicated, may hold values from -5 to 5
- norm_gain: float32 [1024], replicated, may hold values from 0.5 to 1.5
- norm_shift: float32 [1024], replicated, may hold values from -3 to 3
Outputs:
- block_out: bfloat16 [2, 32, 512, 1024], P('rep', 'row', 'col')
- grad_tokens: bfloat16 [2, 32, 512, 1024], P('rep', 'row', 'col')
- grad_qkv_weight: float32 [1024, 3072], P(('rep', 'row', 'col'))
- grad_proj_weight: float32 [1024, 1024], P(('rep', 'row', 'col'))
- grad_qkv_bias: float32 [3072], replicated
- grad_proj_bias: float32 [1024], replicated
- grad_gain: float32 [1024], replicated
- grad_shift: float32 [1024], replicated
- grad_logit_scale: float32 [32], replicated
- grad_position_bias: float32 [32, 64, 64], replicated
The draws below stay inside these ranges and needn't reach their ends.
Inputs may be any that keep to these rules, and one draw needn't show every extreme that they name: `row_field`: field numbers never fall along a slab's rows; a field spans one or more consecutive rows. `col_field`: field numbers never fall along a slab's columns; a field spans one or more consecutive columns.
All inputs are finite; a program needn't handle non-finite values.
Results may differ from the reference program's by a relative error of at most 0.012.
The reference program's roundings to bfloat16 on the way count: a program that leaves them out, or rounds other values in their place, can miss the bound.
Values may be sent and summed in bfloat16 or wider, within the bound.
No kernel may reach another device: no remote copies, remote signals or barrier semaphores. Data moves between devices by JAX's collectives and lax.ppermute only.
A program may use at most 192 MiB of HBM per device.

```python
import math
import jax
import jax.numpy as jnp
import numpy as np
from jax import lax

D = 1024
HEADS = 32
WIN = 8
SHIFT = 4
WIN2 = 64
SLABS = 2
ROWS = 32
COLS = 512


def with_spikes(drawn, stream_key, source, target, shards_of, factor):
    def block_of(dim):
        return (jnp.arange(drawn.shape[dim]) // (drawn.shape[dim] // shards_of)).reshape((-1,) + (1,) * (drawn.ndim - 1 - dim))

    one_side = jax.random.permutation(stream_key, shards_of)[block_of(target)]
    other_side = (block_of(target) + shards_of // 2) % shards_of
    return jnp.where((block_of(source) == one_side) | (block_of(source) == other_side), factor * drawn, drawn)


def block_scale(own_key, dims, cuts, least, high):
    def one(position, parts):
        steps = jax.random.uniform(jax.random.fold_in(jax.random.fold_in(own_key, 6), position), (parts,), jnp.float32, least / len(cuts), high / len(cuts))
        return jnp.repeat(jnp.exp(steps), dims[position] // parts).reshape((-1,) + (1,) * (len(dims) - position - 1))

    factor_of = one(*cuts[0])
    for cut in cuts[1:]:
        factor_of = factor_of * one(*cut)
    return factor_of


def split_up(count, total, most, lean):
    loads = [(1 << 20) // math.isqrt(grade ** lean) + 1 for grade in range(2, count + 1)]
    spare, holding = total - most - (count - 1), [1] * (count - 1)
    while spare > 0:
        candidates = [i for i in range(count - 1) if holding[i] < most]
        mass, budget = sum([loads[i] for i in candidates]), spare
        for i in candidates:
            extra = min(most - holding[i], max(1, budget * loads[i] // mass), spare)
            holding[i] = holding[i] + extra
            spare = spare - extra
    return np.array([most] + holding)


def uneven_parts(own_key, count, total, reach, skew):
    if count == 2:
        one = jax.random.randint(own_key, (), max(1, total - reach), min(reach, total - 1) + 1)
        return jnp.stack([one, total - one])
    tallies = jnp.asarray(split_up(count, total, reach, skew), jnp.int32)
    twos = (count - 1) // 2
    donor, sink = tallies[1:1 + 2 * twos:2], tallies[2:2 + 2 * twos:2]
    room = jnp.minimum(donor - 1, reach - sink)
    passed = jax.random.randint(jax.random.fold_in(own_key, 1), (twos,), 0, 1 << 20) % (room + 1)
    tallies = tallies.at[1:1 + 2 * twos:2].set(donor - passed).at[2:2 + 2 * twos:2].set(sink + passed)
    return tallies[jax.random.permutation(jax.random.fold_in(own_key, 2), count)]


def gaussian(stream_key, dims, deviation, most, shards=(), held_as=jnp.bfloat16):
    values = deviation * jax.random.normal(stream_key, dims, jnp.float32)
    if shards:
        values = values * block_scale(stream_key, dims, shards, -0.22, 0.18)
    return jnp.clip(values, -most, most).astype(held_as)


def gaussian_with(key, dims, width, bound, shards, heavy, dtype=jnp.bfloat16):
    entries = width * jax.random.normal(key, dims, jnp.float32)
    if shards:
        entries = entries * block_scale(key, dims, shards, -0.22, 0.18)
    return jnp.clip(with_spikes(entries, jax.random.fold_in(key, 3), *heavy), -bound, bound).astype(dtype)


def setup_inputs(seed: int = 0) -> dict:
    key_list = jax.random.split(jax.random.key(seed), 13)
    return {
        "tokens": gaussian_with(key_list[0], (SLABS, ROWS, COLS, D), 1.0, 6.0, ((0, 2), (1, 2), (2, 32)), (2, 3, 32, 2.75)),
        "cotangent": gaussian(key_list[1], (SLABS, ROWS, COLS, D), 1.0, 6.0, ((0, 2), (1, 2), (2, 32))),
        "row_field": jax.vmap(lambda own: jnp.searchsorted(jnp.cumsum(uneven_parts(own, ROWS // 4 + 1, ROWS, ROWS // 2, 0)), jnp.arange(ROWS), side="right"))(jax.random.split(key_list[2], SLABS)).reshape((SLABS, ROWS)).astype(jnp.int32),
        "col_field": jax.vmap(lambda own: jnp.searchsorted(jnp.cumsum(uneven_parts(own, COLS // 8, COLS, 16, 1)), jnp.arange(COLS), side="right"))(jax.random.split(key_list[3], SLABS)).reshape((SLABS, COLS)).astype(jnp.int32),
        "qkv_weight": gaussian(key_list[4], (D, 3 * D), D ** -0.5, 0.1875),
        "qkv_bias": gaussian(key_list[5], (3 * D,), 0.5, 3.0, (), jnp.float32),
        "logit_scale": jnp.clip(jnp.exp(jax.random.uniform(key_list[6], (HEADS,), jnp.float32, math.log(2.0), math.log(20.0))), 2.0, 20.0),
        "position_bias": jnp.clip(jax.random.uniform(key_list[7], (HEADS, WIN2, WIN2), jnp.float32, 0.0, 6.0), 0.0, 6.0),
        "proj_weight": gaussian(key_list[8], (D, D), D ** -0.5, 0.1875),
        "proj_bias": gaussian(key_list[9], (D,), 1.0, 5.0, (), jnp.float32),
        "norm_gain": jnp.clip(1.0 + 0.1 * jax.random.normal(key_list[10], (D,), jnp.float32), 0.5, 1.5),
        "norm_shift": gaussian(key_list[11], (D,), 0.5, 3.0, (), jnp.float32),
    }


norm_epsilon = 1e-05
unit_floor = 1e-12

def to_windows(values, row_count, col_count, window):
    pieces, head_count, head_size = (values.shape[1], values.shape[2], values.shape[3])
    values = values.reshape(row_count // window, window, col_count // window, window, pieces, head_count, head_size)
    values = values.transpose(0, 2, 4, 5, 1, 3, 6)
    return values.reshape(row_count // window * (col_count // window), pieces, head_count, window * window, head_size)

def from_windows(values, row_count, col_count, window):
    pieces, head_count, head_size = (values.shape[1], values.shape[2], values.shape[4])
    values = values.reshape(row_count // window, col_count // window, pieces, head_count, window, window, head_size)
    values = values.transpose(0, 4, 1, 5, 2, 3, 6)
    return values.reshape(row_count * col_count, pieces * head_count * head_size)

def unit_rows(raw_rows):
    length = jnp.sqrt(lax.optimization_barrier(jnp.sum(raw_rows * raw_rows, axis=-1, keepdims=True)))
    scale_back = 1.0 / jnp.maximum(length, unit_floor)
    return (raw_rows * scale_back, scale_back)

def field_mask(row_ids, col_ids, window):
    row_blocks = row_ids.reshape(-1, window)
    col_blocks = col_ids.reshape(-1, window)
    grid_shape = (row_blocks.shape[0], col_blocks.shape[0], window, window)
    row_token = jnp.broadcast_to(row_blocks[:, None, :, None], grid_shape).reshape(-1, window * window)
    col_token = jnp.broadcast_to(col_blocks[None, :, None, :], grid_shape).reshape(-1, window * window)
    allowed = (row_token[:, :, None] == row_token[:, None, :]) & (col_token[:, :, None] == col_token[:, None, :])
    return allowed.astype(jnp.float32)[:, None]

def block_step(shifted, grad_branch, row_ids, col_ids, qkv_weight, qkv_bias, logit_scale, position_bias, proj_weight, proj_bias, norm_gain, norm_shift):
    row_count, col_count, model_width = shifted.shape
    window = WIN
    head_size = model_width // HEADS
    flat_rows = shifted.reshape(row_count * col_count, model_width)
    qkv_rows = (jnp.dot(flat_rows, qkv_weight, preferred_element_type=jnp.float32) + qkv_bias).astype(jnp.bfloat16)
    windows = to_windows(qkv_rows.reshape(-1, 3, HEADS, head_size), row_count, col_count, window)
    query_raw = windows[:, 0].astype(jnp.float32)
    key_raw = windows[:, 1].astype(jnp.float32)
    value_win = windows[:, 2]
    query_unit, query_inv = unit_rows(query_raw)
    key_unit, key_inv = unit_rows(key_raw)
    query_cast = query_unit.astype(jnp.bfloat16)
    key_cast = key_unit.astype(jnp.bfloat16)
    cosine = jnp.einsum('nhid,nhjd->nhij', query_cast.astype(jnp.float32), key_cast.astype(jnp.float32))
    scores = logit_scale[None, :, None, None] * cosine + position_bias[None]
    allowed = field_mask(row_ids, col_ids, window)
    weights = jnp.exp(scores) * allowed
    totals = lax.optimization_barrier(jnp.sum(weights, axis=-1, keepdims=True))
    attention = (weights / totals).astype(jnp.bfloat16)
    attention_f = attention.astype(jnp.float32)
    attended = jnp.einsum('nhij,nhjd->nhid', attention_f, value_win.astype(jnp.float32)).astype(jnp.bfloat16)
    mixed_flat = from_windows(attended[:, None], row_count, col_count, window)
    projected = jnp.dot(mixed_flat, proj_weight, preferred_element_type=jnp.float32) + proj_bias
    centre = projected - lax.optimization_barrier(jnp.mean(projected, axis=-1, keepdims=True))
    variance = lax.optimization_barrier(jnp.mean(centre * centre, axis=-1, keepdims=True))
    inv_std = lax.rsqrt(variance + norm_epsilon)
    normed = centre * inv_std
    branch = (normed * norm_gain + norm_shift).astype(jnp.bfloat16)
    grad_out = grad_branch.reshape(row_count * col_count, model_width).astype(jnp.float32)
    sum_gain = lax.optimization_barrier(jnp.sum(grad_out * normed, axis=0))
    sum_shift = lax.optimization_barrier(jnp.sum(grad_out, axis=0))
    grad_normed = grad_out * norm_gain
    grad_projected = inv_std * (grad_normed - lax.optimization_barrier(jnp.mean(grad_normed, axis=-1, keepdims=True)) - normed * lax.optimization_barrier(jnp.mean(grad_normed * normed, axis=-1, keepdims=True)))
    sum_proj_bias = lax.optimization_barrier(jnp.sum(grad_projected, axis=0))
    grad_projected_low = grad_projected.astype(jnp.bfloat16)
    grad_mixed = jnp.dot(grad_projected_low, proj_weight.T, preferred_element_type=jnp.float32).astype(jnp.bfloat16)
    grad_win = to_windows(grad_mixed.reshape(-1, 1, HEADS, head_size), row_count, col_count, window)[:, 0]
    grad_win_f = grad_win.astype(jnp.float32)
    grad_attention = jnp.einsum('nhid,nhjd->nhij', grad_win_f, value_win.astype(jnp.float32))
    grad_value = jnp.einsum('nhij,nhid->nhjd', attention_f, grad_win_f)
    grad_scores = attention_f * (grad_attention - lax.optimization_barrier(jnp.sum(grad_attention * attention_f, axis=-1, keepdims=True)))
    sum_scale = lax.optimization_barrier(jnp.sum(grad_scores * cosine, axis=(0, 2, 3)))
    sum_bias = lax.optimization_barrier(jnp.sum(grad_scores, axis=0))
    grad_cosine = (logit_scale[None, :, None, None] * grad_scores).astype(jnp.bfloat16).astype(jnp.float32)
    grad_query_unit = jnp.einsum('nhij,nhjd->nhid', grad_cosine, key_cast.astype(jnp.float32))
    grad_key_unit = jnp.einsum('nhij,nhid->nhjd', grad_cosine, query_cast.astype(jnp.float32))
    grad_query = query_inv * grad_query_unit - query_raw * query_inv ** 3 * lax.optimization_barrier(jnp.sum(grad_query_unit * query_raw, axis=-1, keepdims=True))
    grad_key = key_inv * grad_key_unit - key_raw * key_inv ** 3 * lax.optimization_barrier(jnp.sum(grad_key_unit * key_raw, axis=-1, keepdims=True))
    grad_windows = jnp.stack((grad_query, grad_key, grad_value), axis=1)
    grad_qkv = from_windows(grad_windows, row_count, col_count, window)
    sum_qkv_bias = lax.optimization_barrier(jnp.sum(grad_qkv, axis=0))
    grad_qkv_low = grad_qkv.astype(jnp.bfloat16)
    grad_shifted = jnp.dot(grad_qkv_low, qkv_weight.T, preferred_element_type=jnp.float32).astype(jnp.bfloat16)
    partial_sums = (sum_bias, sum_scale, sum_qkv_bias, sum_proj_bias, sum_gain, sum_shift)
    return (branch.reshape(row_count, col_count, model_width), grad_shifted.reshape(row_count, col_count, model_width), flat_rows, mixed_flat, grad_projected_low, grad_qkv_low, partial_sums)

def reference(tokens, cotangent, row_field, col_field, qkv_weight, qkv_bias, logit_scale, position_bias, proj_weight, proj_bias, norm_gain, norm_shift):
    shifted = jnp.roll(tokens, (-SHIFT, -SHIFT), axis=(1, 2))
    grad_shifted_in = jnp.roll(cotangent, (-SHIFT, -SHIFT), axis=(1, 2))
    row_moved = jnp.roll(row_field, -SHIFT, axis=1)
    col_moved = jnp.roll(col_field, -SHIFT, axis=1)
    band_count = SLABS * ROWS // WIN
    bands = shifted.reshape(band_count, WIN, COLS, D)
    grad_bands = grad_shifted_in.reshape(band_count, WIN, COLS, D)
    row_bands = row_moved.reshape(band_count, WIN)
    col_bands = jnp.repeat(col_moved, ROWS // WIN, axis=0)
    initial = (jnp.zeros((D, 4 * D), jnp.float32), jnp.zeros((HEADS, WIN2, WIN2), jnp.float32), jnp.zeros((HEADS,), jnp.float32), jnp.zeros((3 * D,), jnp.float32), jnp.zeros((D,), jnp.float32), jnp.zeros((D,), jnp.float32), jnp.zeros((D,), jnp.float32))

    def one_band(running, band_items):
        band_rows, grad_band, row_ids, col_ids = band_items
        branch, grad_band_x, flat_rows, mixed_flat, grad_projected_low, grad_qkv_low, partial_sums = block_step(band_rows, grad_band, row_ids, col_ids, qkv_weight, qkv_bias, logit_scale, position_bias, proj_weight, proj_bias, norm_gain, norm_shift)
        grad_term = jnp.concatenate((jnp.dot(flat_rows.T, grad_qkv_low, preferred_element_type=jnp.float32), jnp.dot(mixed_flat.T, grad_projected_low, preferred_element_type=jnp.float32)), axis=1)
        updated = (running[0] + grad_term,) + tuple((old_sum + new_sum for old_sum, new_sum in zip(running[1:], partial_sums)))
        return (updated, (branch, grad_band_x))
    totals, (branches, grad_pieces) = lax.scan(one_band, initial, (bands, grad_bands, row_bands, col_bands))
    returned = jnp.roll(branches.reshape(SLABS, ROWS, COLS, D), (SHIFT, SHIFT), axis=(1, 2))
    grad_returned = jnp.roll(grad_pieces.reshape(SLABS, ROWS, COLS, D), (SHIFT, SHIFT), axis=(1, 2))
    block_out = (tokens.astype(jnp.float32) + returned.astype(jnp.float32)).astype(jnp.bfloat16)
    grad_tokens = (cotangent.astype(jnp.float32) + grad_returned.astype(jnp.float32)).astype(jnp.bfloat16)
    return (block_out, grad_tokens, totals[0][:, :3 * D], totals[0][:, 3 * D:], totals[3], totals[4], totals[5], totals[6], totals[2], totals[1])
```

```python
import functools

import jax
import jax.numpy as jnp
import numpy as np
from jax import lax
from jax.experimental import pallas as pl
from jax.experimental.pallas import tpu as pltpu
from jax.sharding import PartitionSpec as P

HEADS = 32
WIN = 8
SHIFT = 4
SIDE = 16
TOK = SIDE * SIDE
D = 1024
HALO = SIDE * SHIFT
CORNER = SHIFT * SHIFT
CAT = TOK + 2 * HALO + CORNER
WIN2 = WIN * WIN
WINDOWS = TOK // WIN2
GROUP = 4
GROUPS = HEADS // GROUP
LANES = 128
WIDE = GROUP * WIN2
AXES = ("rep", "row", "col")

norm_epsilon = 1e-05
unit_floor = 1e-12
f32 = jnp.float32
bf16 = jnp.bfloat16
VMEM_LIMIT = 56 * 1024 * 1024


def window_order():
    order = np.zeros((TOK, CAT), np.float32)
    for r in range(SIDE):
        for c in range(SIDE):
            n = ((r // WIN) * 2 + c // WIN) * WIN2 + (r % WIN) * WIN + c % WIN
            rr, cc = r + SHIFT, c + SHIFT
            if rr < SIDE and cc < SIDE:
                m = rr * SIDE + cc
            elif cc < SIDE:
                m = TOK + (rr - SIDE) * SIDE + cc
            elif rr < SIDE:
                m = TOK + HALO + rr * SHIFT + (cc - SIDE)
            else:
                m = TOK + 2 * HALO + (rr - SIDE) * SHIFT + (cc - SIDE)
            order[n, m] = 1.0
    return order


def border_spread():
    spread = np.zeros((TOK, HALO + CORNER), np.float32)
    for r in range(SIDE):
        for c in range(SHIFT):
            spread[r * SIDE + c, r * SHIFT + c] = 1.0
    for r in range(SHIFT):
        for c in range(SHIFT):
            spread[r * SIDE + c, HALO + r * SHIFT + c] = 1.0
    return spread


def head_mask():
    rows = np.arange(WIDE)[:, None] // WIN2
    cols = np.arange(LANES)[None, :] // (LANES // GROUP)
    return (rows == cols).astype(np.float32)


def head_sums():
    a = np.arange(2 * LANES)[:, None] % LANES // (LANES // GROUP)
    b = np.arange(LANES)[None, :] // (LANES // GROUP)
    return (a == b).astype(np.float32)


def mm(a, b):
    return jnp.dot(a, b, preferred_element_type=f32)


def mm_tb(a, b):
    return lax.dot_general(a, b, (((1,), (1,)), ((), ())), preferred_element_type=f32)


def mm_ta(a, b):
    return lax.dot_general(a, b, (((0,), (0,)), ((), ())), preferred_element_type=f32)


def segment_sums(values, ones):
    high = values.astype(bf16)
    low = (values - high.astype(f32)).astype(bf16)
    return mm(jnp.concatenate((high, low), axis=1), ones)


def inverse_length(raw, ones):
    total = segment_sums(raw * raw, ones)
    return 1.0 / jnp.maximum(jnp.sqrt(total), unit_floor)


def stacked_heads(x, mask):
    return jnp.concatenate((x, x, x, x), axis=0) * mask


def own_heads(wide, mask):
    out = wide[:WIN2] * mask[:WIN2].astype(f32)
    for h in range(1, GROUP):
        out = out + wide[h * WIN2 : (h + 1) * WIN2] * mask[h * WIN2 : (h + 1) * WIN2].astype(f32)
    return out


def forward_kernel(
    fields, tok, tok_row, tok_col, tok_cor, cot, cot_row, cot_col, cot_cor, order, order_t, mask_ref, ones_ref,
    wqkv, bqkv, scale, bias_t, wproj, bproj, gain, shift,
    x_out, qkv, att, mixed, gp, b_own, b_row, b_col, b_cor, sums, cat, branch, grad,
):
    cat[0:TOK] = tok[...]
    cat[TOK : TOK + HALO] = tok_row[...]
    cat[TOK + HALO : TOK + 2 * HALO] = tok_col[...]
    cat[TOK + 2 * HALO : CAT] = tok_cor[...]
    x_out[...] = mm(order[...], cat[...]).astype(bf16)
    cat[0:TOK] = cot[...]
    cat[TOK : TOK + HALO] = cot_row[...]
    cat[TOK + HALO : TOK + 2 * HALO] = cot_col[...]
    cat[TOK + 2 * HALO : CAT] = cot_cor[...]
    grad[...] = mm(order[...], cat[...]).astype(bf16)

    @pl.loop(0, 3 * D // 512)
    def _(n):
        cols = pl.ds(pl.multiple_of(n * 512, 512), 512)
        qkv[:, cols] = (mm(x_out[...], wqkv[:, cols]) + bqkv[:, cols]).astype(bf16)

    sub = lax.broadcasted_iota(jnp.int32, (WIN2, WIDE), 0)
    lane = lax.broadcasted_iota(jnp.int32, (WIN2, WIDE), 1) % WIN2
    allowed = []
    for w in range(WINDOWS):
        id_sub = jnp.zeros((WIN2, WIDE), jnp.int32)
        id_lane = jnp.zeros((WIN2, WIDE), jnp.int32)
        for i in range(WIN):
            rid = fields[0, (w // 2) * WIN + i] * 1024
            cid = fields[1, (w % 2) * WIN + i]
            id_sub = id_sub + jnp.where(sub // WIN == i, rid, 0) + jnp.where(sub % WIN == i, cid, 0)
            id_lane = id_lane + jnp.where(lane // WIN == i, rid, 0) + jnp.where(lane % WIN == i, cid, 0)
        allowed.append((id_sub == id_lane).astype(f32))
    mask = mask_ref[...]
    ones = ones_ref[...]

    @pl.loop(0, GROUPS)
    def _(g):
        at = pl.multiple_of(g * LANES, LANES)
        qs = pl.ds(at, LANES)
        ks = pl.ds(at + D, LANES)
        vs = pl.ds(at + 2 * D, LANES)
        q = qkv[:, qs].astype(f32)
        k = qkv[:, ks].astype(f32)
        v = qkv[:, vs]
        qu = (q * inverse_length(q, ones)).astype(bf16)
        ku = (k * inverse_length(k, ones)).astype(bf16)
        sc = scale[pl.ds(g, 1), :]
        bias = bias_t[g]
        for w in range(WINDOWS):
            rows = slice(w * WIN2, (w + 1) * WIN2)
            cosine = mm_tb(ku[rows], stacked_heads(qu[rows], mask))
            weights = jnp.exp(sc * cosine + bias) * allowed[w]
            total = jnp.sum(weights, axis=0, keepdims=True)
            attention = (weights * (1.0 / total)).astype(bf16)
            att[g, w] = attention
            mixed[rows, qs] = own_heads(mm_ta(attention, v[rows]), mask).astype(bf16)

    gain_v = gain[...]
    shift_v = shift[...]
    sums[...] = jnp.zeros_like(sums)
    for w in range(WINDOWS):
        rows = slice(w * WIN2, (w + 1) * WIN2)
        projected = mm(mixed[rows, :], wproj[...]) + bproj[...]
        centre = projected - jnp.mean(projected, axis=-1, keepdims=True)
        inv_std = lax.rsqrt(jnp.mean(centre * centre, axis=-1, keepdims=True) + norm_epsilon)
        normed = centre * inv_std
        branch[rows, :] = (normed * gain_v + shift_v).astype(bf16)
        go = grad[rows, :].astype(f32)
        gn = go * gain_v
        gpf = inv_std * (
            gn - jnp.mean(gn, axis=-1, keepdims=True) - normed * jnp.mean(gn * normed, axis=-1, keepdims=True)
        )
        gp[rows, :] = gpf.astype(bf16)
        sums[0:1, :] += jnp.sum(gpf, axis=0, keepdims=True)
        sums[1:2, :] += jnp.sum(go * normed, axis=0, keepdims=True)
        sums[2:3, :] += jnp.sum(go, axis=0, keepdims=True)
    put_back(order_t, branch, b_own, b_row, b_col, b_cor)


def put_back(order_t, source, own, row, col, cor):
    src = source[...]
    own[...] = mm(order_t[0:TOK], src).astype(bf16)
    row[...] = mm(order_t[TOK : TOK + HALO], src).astype(bf16)
    col[...] = mm(order_t[TOK + HALO : TOK + 2 * HALO], src).astype(bf16)
    cor[...] = mm(order_t[TOK + 2 * HALO : CAT], src).astype(bf16)


def attention_grad_kernel(
    half, qkv, att, gp, wproj, scale, mask_ref, ones_ref, g_keep, g_send, pos, scale_sums, bias_sums, gm
):
    p = half[0]
    gm[...] = mm_tb(gp[...], wproj[...]).astype(bf16)
    mask = mask_ref[...]
    ones = ones_ref[...]

    @pl.loop(0, GROUPS)
    def _(g):
        at = pl.multiple_of(g * LANES, LANES)
        qs = pl.ds(at, LANES)
        ks = pl.ds(at + D, LANES)
        vs = pl.ds(at + 2 * D, LANES)
        q = qkv[:, qs].astype(f32)
        k = qkv[:, ks].astype(f32)
        v = qkv[:, vs]
        q_inv = inverse_length(q, ones)
        k_inv = inverse_length(k, ones)
        qu = (q * q_inv).astype(bf16)
        ku = (k * k_inv).astype(bf16)
        gmx = gm[:, qs]
        sc = scale[pl.ds(g, 1), :]
        pos_sum = jnp.zeros((WIN2, WIDE), f32)
        sc_sum = jnp.zeros((1, WIDE), f32)
        gqu, gku, gv = [], [], []
        for w in range(WINDOWS):
            rows = slice(w * WIN2, (w + 1) * WIN2)
            q_heads = stacked_heads(qu[rows], mask)
            g_heads = stacked_heads(gmx[rows], mask)
            cosine = mm_tb(ku[rows], q_heads)
            grad_att = mm_tb(v[rows], g_heads)
            attention = att[g, w]
            gv.append(mm(attention, g_heads))
            att_f = attention.astype(f32)
            dots = jnp.sum(grad_att * att_f, axis=0, keepdims=True)
            grad_scores = att_f * (grad_att - dots)
            pos_sum = pos_sum + grad_scores
            sc_sum = sc_sum + jnp.sum(grad_scores * cosine, axis=0, keepdims=True)
            grad_cos = (sc * grad_scores).astype(bf16)
            gku.append(mm(grad_cos, q_heads))
            gqu.append(own_heads(mm_ta(grad_cos, ku[rows]), mask))
        scale_sums[pl.ds(g, 1), :] = sc_sum
        pos[pl.ds(pl.multiple_of(g * WIDE, WIDE), WIDE), :] = pos_sum.T
        gqu = jnp.concatenate(gqu, axis=0)
        gku = jnp.concatenate(gku, axis=0)
        gvf = jnp.concatenate(gv, axis=0)
        gqf = q_inv * gqu - q * (q_inv * q_inv * q_inv) * segment_sums(gqu * q, ones)
        gkf = k_inv * gku - k * (k_inv * k_inv * k_inv) * segment_sums(gku * k, ones)
        bias_sums[0:1, qs] = jnp.sum(gqf, axis=0, keepdims=True)
        bias_sums[1:2, qs] = jnp.sum(gkf, axis=0, keepdims=True)
        bias_sums[2:3, qs] = jnp.sum(gvf, axis=0, keepdims=True)
        side = g // (GROUPS // 2)
        inner = pl.multiple_of((g - side * (GROUPS // 2)) * LANES, LANES)

        def put(ref):
            ref[:, pl.ds(inner, LANES)] = gqf.astype(bf16)
            ref[:, pl.ds(inner + D // 2, LANES)] = gkf.astype(bf16)
            ref[:, pl.ds(inner + D, LANES)] = gvf.astype(bf16)

        pl.when(side == p)(lambda: put(g_keep))
        pl.when(side != p)(lambda: put(g_send))


def input_grad_kernel(half, g_keep, g_send, wqkv, order_t, s_own, s_row, s_col, s_cor, total):
    p = half[0]
    for t in range(3):
        for ref, side in ((g_keep, p), (g_send, 1 - p)):
            cols = pl.ds(pl.multiple_of(t * D + side * (D // 2), D // 2), D // 2)
            term = mm_tb(ref[:, t * (D // 2) : (t + 1) * (D // 2)], wqkv[:, cols])
            if t == 0 and ref is g_keep:
                total[...] = term
            else:
                total[...] += term
    gs = total[...].astype(bf16)
    s_own[...] = mm(order_t[0:TOK], gs).astype(bf16)
    s_row[...] = mm(order_t[TOK : TOK + HALO], gs).astype(bf16)
    s_col[...] = mm(order_t[TOK + HALO : TOK + 2 * HALO], gs).astype(bf16)
    s_cor[...] = mm(order_t[TOK + 2 * HALO : CAT], gs).astype(bf16)


def weight_grad_kernel(a_own, a_other, g_own, g_other, out):
    a = jnp.concatenate((a_own[...], a_other[...]), axis=0)
    g = jnp.concatenate((g_own[...], g_other[...]), axis=0)
    out[...] = mm_ta(a, g).astype(bf16)


def finish_kernel(base, own, row, col, cor, spread, out):
    border = jnp.concatenate((col[...], cor[...]), axis=0)
    moved = own[...].astype(f32) + mm(spread[...], border)
    total = base[...].astype(f32) + moved
    out[HALO:, :] = total[HALO:].astype(bf16)
    out[:HALO, :] = (total[:HALO] + row[...].astype(f32)).astype(bf16)


def sds(shape, dtype):
    return jax.ShapeDtypeStruct(shape, dtype)


VM = pl.BlockSpec(memory_space=pltpu.VMEM)
SM = pl.BlockSpec(memory_space=pltpu.SMEM)


def call(kernel, outs, scratch=(), specs=None, flops=0, bytes_accessed=0):
    return pl.pallas_call(
        kernel,
        out_shape=outs,
        in_specs=specs,
        out_specs=jax.tree.map(lambda _: VM, outs),
        scratch_shapes=list(scratch),
        compiler_params=pltpu.CompilerParams(vmem_limit_bytes=VMEM_LIMIT),
        cost_estimate=pl.CostEstimate(flops=flops, bytes_accessed=bytes_accessed, transcendentals=0),
    )


def neighbour(by_row, by_col):
    rows, cols = lax.axis_size("row"), lax.axis_size("col")
    reps = lax.axis_size("rep")
    pairs = []
    for s in range(reps):
        for r in range(rows):
            for c in range(cols):
                to = (s * rows + (r + by_row) % rows) * cols + (c + by_col) % cols
                pairs.append(((s * rows + r) * cols + c, to))
    return pairs


def swap_cores(x):
    size = lax.axis_size("col")
    return lax.ppermute(x, "col", [(i, i ^ 1) for i in range(size)])


def weight_grad(a_own, a_other, g_own, g_other):
    width = g_own.shape[1]
    block = 256
    return pl.pallas_call(
        weight_grad_kernel,
        grid=(D // block,),
        out_shape=sds((D, width), bf16),
        in_specs=[
            pl.BlockSpec((TOK, block), lambda i: (0, i)),
            pl.BlockSpec((TOK, block), lambda i: (0, i)),
            pl.BlockSpec((TOK, width), lambda i: (0, 0)),
            pl.BlockSpec((TOK, width), lambda i: (0, 0)),
        ],
        out_specs=pl.BlockSpec((block, width), lambda i: (i, 0)),
        compiler_params=pltpu.CompilerParams(vmem_limit_bytes=VMEM_LIMIT),
        cost_estimate=pl.CostEstimate(flops=4 * TOK * D * width, bytes_accessed=4 * D * width, transcendentals=0),
    )(a_own, a_other, g_own, g_other)


def per_device(
    tokens, cotangent, row_field, col_field, qkv_weight, qkv_bias, logit_scale, position_bias,
    proj_weight, proj_bias, norm_gain, norm_shift,
):
    devices = lax.axis_size(AXES)
    order = jnp.asarray(window_order(), bf16)
    order_t = jnp.asarray(window_order().T, bf16)
    spread = jnp.asarray(border_spread(), bf16)
    mask = jnp.asarray(head_mask(), bf16)
    ones = jnp.asarray(head_sums(), bf16)

    both = jnp.stack((tokens[0], cotangent[0]))
    row_in = lax.ppermute(both[:, :SHIFT].reshape(2, HALO, D), AXES, neighbour(-1, 0))
    col_in = lax.ppermute(both[:, :, :SHIFT].reshape(2, HALO, D), AXES, neighbour(0, -1))
    cor_in = lax.ppermute(both[:, :SHIFT, :SHIFT].reshape(2, CORNER, D), AXES, neighbour(-1, -1))

    row_ids = lax.dynamic_slice_in_dim(jnp.roll(row_field[0], -SHIFT), lax.axis_index("row") * SIDE, SIDE)
    col_ids = lax.dynamic_slice_in_dim(jnp.roll(col_field[0], -SHIFT), lax.axis_index("col") * SIDE, SIDE)
    fields = jnp.stack((row_ids, col_ids))
    half = (lax.axis_index("col") % 2).astype(jnp.int32).reshape(1)
    scale = jnp.repeat(logit_scale, WIN2).reshape(GROUPS, WIDE)
    bias_t = position_bias.reshape(GROUPS, GROUP, WIN2, WIN2).transpose(0, 3, 1, 2).reshape(GROUPS, WIN2, WIDE)
    tok = tokens[0].reshape(TOK, D)
    cot = cotangent[0].reshape(TOK, D)

    x, qkv, att, mixed, gp, b_own, b_row, b_col, b_cor, sums = call(
        forward_kernel,
        (
            sds((TOK, D), bf16), sds((TOK, 3 * D), bf16), sds((GROUPS, WINDOWS, WIN2, WIDE), bf16),
            sds((TOK, D), bf16), sds((TOK, D), bf16), sds((TOK, D), bf16), sds((HALO, D), bf16),
            sds((HALO, D), bf16), sds((CORNER, D), bf16), sds((8, D), f32),
        ),
        [pltpu.VMEM((CAT, D), bf16), pltpu.VMEM((TOK, D), bf16), pltpu.VMEM((TOK, D), bf16)],
        [SM] + [VM] * 20,
        flops=3 * 10**9, bytes_accessed=16 * 2**20,
    )(
        fields, tok, row_in[0], col_in[0], cor_in[0], cot, row_in[1], col_in[1], cor_in[1],
        order, order_t, mask, ones, qkv_weight, qkv_bias.reshape(1, -1), scale, bias_t,
        proj_weight, proj_bias.reshape(1, -1), norm_gain.reshape(1, -1), norm_shift.reshape(1, -1),
    )
    x_other = swap_cores(x)
    mixed_other = swap_cores(mixed)
    gp_keep = lax.dynamic_slice_in_dim(gp, half[0] * (D // 2), D // 2, axis=1)
    gp_send = lax.dynamic_slice_in_dim(gp, (1 - half[0]) * (D // 2), D // 2, axis=1)
    gp_other = swap_cores(gp_send)
    proj_part = weight_grad(mixed, mixed_other, gp_keep, gp_other)
    proj_got = lax.all_to_all(proj_part.reshape(devices, -1, D // 2), AXES, 0, 0, tiled=True)

    def sent_back(own, row, col, cor, base):
        row = lax.ppermute(row, AXES, neighbour(1, 0))
        col = lax.ppermute(col, AXES, neighbour(0, 1))
        cor = lax.ppermute(cor, AXES, neighbour(1, 1))
        out = call(finish_kernel, sds((TOK, D), bf16), (), [VM] * 6, flops=10**8, bytes_accessed=2**21)(
            base, own, row, col, cor, spread
        )
        return out.reshape(1, SIDE, SIDE, D)

    block_out = sent_back(b_own, b_row, b_col, b_cor, tok)

    g_keep, g_send, pos, scale_sums, bias_sums = call(
        attention_grad_kernel,
        (
            sds((TOK, 3 * D // 2), bf16), sds((TOK, 3 * D // 2), bf16), sds((HEADS * WIN2, WIN2), f32),
            sds((GROUPS, WIDE), f32), sds((8, D), f32),
        ),
        [pltpu.VMEM((TOK, D), bf16)],
        [SM] + [VM] * 7,
        flops=10**9, bytes_accessed=8 * 2**20,
    )(half, qkv, att, gp, proj_weight, scale, mask, ones)
    g_other = swap_cores(g_send)
    qkv_part = weight_grad(x, x_other, g_keep, g_other)
    qkv_got = lax.all_to_all(qkv_part.reshape(devices, -1, 3 * D // 2), AXES, 0, 0, tiled=True)

    vector = jnp.concatenate((
        bias_sums[:3].reshape(-1), sums[:3].reshape(-1), scale_sums.reshape(HEADS, WIN2).sum(axis=1),
        jnp.zeros(8192 - 6 * D - HEADS, f32),
    ))
    vec_rows = 128 // devices
    pos_rows = HEADS * WIN2 // devices
    vector = jnp.pad(vector.reshape(devices, vec_rows, 64), ((0, 0), (0, pos_rows - vec_rows), (0, 0)))
    small = jnp.concatenate((pos.reshape(devices, pos_rows, WIN2), vector), axis=2).astype(bf16)
    small = lax.all_to_all(small, AXES, 0, 0, tiled=True)
    small = jnp.sum(small.astype(f32), axis=0).astype(bf16)
    small = lax.all_to_all(jnp.broadcast_to(small[None], (devices,) + small.shape), AXES, 0, 0, tiled=True)
    grad_position = small[:, :, :WIN2].astype(f32).reshape(HEADS, WIN2, WIN2)
    vector = small[:, :vec_rows, WIN2:].astype(f32).reshape(-1)

    s_own, s_row, s_col, s_cor = call(
        input_grad_kernel,
        (sds((TOK, D), bf16), sds((HALO, D), bf16), sds((HALO, D), bf16), sds((CORNER, D), bf16)),
        [pltpu.VMEM((TOK, D), f32)],
        [SM] + [VM] * 4,
        flops=2 * 10**9, bytes_accessed=9 * 2**20,
    )(half, g_keep, g_send, qkv_weight, order_t)
    grad_tokens = sent_back(s_own, s_row, s_col, s_cor, cot)

    def summed(got, width):
        total = jnp.sum(got.astype(f32).reshape(devices // 2, 2, -1, got.shape[-1]), axis=0)
        parts = total.reshape(2, total.shape[1], -1, D // 2)
        return parts.transpose(1, 2, 0, 3).reshape(total.shape[1], width)

    grad_qkv_weight = summed(qkv_got, 3 * D)
    grad_proj_weight = summed(proj_got, D)
    return (
        block_out, grad_tokens, grad_qkv_weight, grad_proj_weight, vector[: 3 * D], vector[3 * D : 4 * D],
        vector[4 * D : 5 * D], vector[5 * D : 6 * D], vector[6 * D : 6 * D + HEADS], grad_position,
    )


def solution(mesh):
    grid = P("rep", "row", "col", None)
    rows = P(AXES, None)
    return jax.shard_map(
        per_device,
        mesh=mesh,
        in_specs=(grid, grid, P("rep", None), P("rep", None)) + (P(),) * 8,
        out_specs=(grid, grid, rows, rows) + (P(),) * 6,
        check_vma=False,
    )
```

```python
import functools

import jax
import jax.numpy as jnp
import numpy as np
from jax import lax
from jax.experimental import pallas as pl
from jax.experimental.pallas import tpu as pltpu
from jax.sharding import PartitionSpec as P

HEADS = 32
WIN = 8
SHIFT = 4
SIDE = 16
TOK = SIDE * SIDE
D = 1024
HALO = SIDE * SHIFT
CORNER = SHIFT * SHIFT
CAT = TOK + 2 * HALO + CORNER
WIN2 = WIN * WIN
WINDOWS = TOK // WIN2
GROUP = 4
GROUPS = HEADS // GROUP
LANES = 128
WIDE = GROUP * WIN2
AXES = ("rep", "row", "col")

norm_epsilon = 1e-05
unit_floor = 1e-12
f32 = jnp.float32
bf16 = jnp.bfloat16
VMEM_LIMIT = 56 * 1024 * 1024


def window_order():
    order = np.zeros((TOK, CAT), np.float32)
    for r in range(SIDE):
        for c in range(SIDE):
            n = ((r // WIN) * 2 + c // WIN) * WIN2 + (r % WIN) * WIN + c % WIN
            rr, cc = r + SHIFT, c + SHIFT
            if rr < SIDE and cc < SIDE:
                m = rr * SIDE + cc
            elif cc < SIDE:
                m = TOK + (rr - SIDE) * SIDE + cc
            elif rr < SIDE:
                m = TOK + HALO + rr * SHIFT + (cc - SIDE)
            else:
                m = TOK + 2 * HALO + (rr - SIDE) * SHIFT + (cc - SIDE)
            order[n, m] = 1.0
    return order


def border_spread():
    spread = np.zeros((TOK, HALO + CORNER), np.float32)
    for r in range(SIDE):
        for c in range(SHIFT):
            spread[r * SIDE + c, r * SHIFT + c] = 1.0
    for r in range(SHIFT):
        for c in range(SHIFT):
            spread[r * SIDE + c, HALO + r * SHIFT + c] = 1.0
    return spread


def head_mask():
    rows = np.arange(WIDE)[:, None] // WIN2
    cols = np.arange(LANES)[None, :] // (LANES // GROUP)
    return (rows == cols).astype(np.float32)


def head_sums():
    a = np.arange(2 * LANES)[:, None] % LANES // (LANES // GROUP)
    b = np.arange(LANES)[None, :] // (LANES // GROUP)
    return (a == b).astype(np.float32)


def mm(a, b):
    return jnp.dot(a, b, preferred_element_type=f32)


def mm_tb(a, b):
    return lax.dot_general(a, b, (((1,), (1,)), ((), ())), preferred_element_type=f32)


def mm_ta(a, b):
    return lax.dot_general(a, b, (((0,), (0,)), ((), ())), preferred_element_type=f32)


def segment_sums(values, ones):
    high = values.astype(bf16)
    low = (values - high.astype(f32)).astype(bf16)
    return mm(jnp.concatenate((high, low), axis=1), ones)


def inverse_length(raw, ones):
    total = segment_sums(raw * raw, ones)
    return 1.0 / jnp.maximum(jnp.sqrt(total), unit_floor)


def stacked_heads(x, mask):
    return jnp.concatenate((x, x, x, x), axis=0) * mask


def pack_kernel(tok, cot, spread_t, row, col, cor):
    for n, ref in enumerate((tok, cot)):
        border = mm(spread_t[...], ref[...]).astype(bf16)
        row[n] = ref[0:HALO, :]
        col[n] = border[:HALO]
        cor[n] = border[HALO:]


def put_back(order_t, src, own, row, col, cor):
    own[...] = mm(order_t[0:TOK], src).astype(bf16)
    row[...] = mm(order_t[TOK : TOK + HALO], src).astype(bf16)
    col[...] = mm(order_t[TOK + HALO : TOK + 2 * HALO], src).astype(bf16)
    cor[...] = mm(order_t[TOK + 2 * HALO : CAT], src).astype(bf16)


def local_kernel(
    place, row_field, col_field, logit_scale, tok, cot, row_in, col_in, cor_in, order, order_t, mask_ref, ones_ref,
    wqkv_hbm, bqkv, bias_hbm, wproj_hbm, bproj, gain, shift,
    keep, send, b_own, b_row, b_col, b_cor, small,
    wqkv, wproj, bias_t, cat, qkv, att, units, inverses, grad, wide, branch, pos, vec, sems,
):
    loads = [
        pltpu.make_async_copy(wqkv_hbm.at[:, pl.ds(t * D, D)], wqkv.at[:, pl.ds(t * D, D)], sems.at[t])
        for t in range(3)
    ]
    loads.append(pltpu.make_async_copy(bias_hbm, bias_t, sems.at[3]))
    loads.append(pltpu.make_async_copy(wproj_hbm, wproj, sems.at[4]))
    for load in loads:
        load.start()

    p = place[2]
    mixed_at, gp_at, g_at = D, 2 * D, 2 * D + D // 2
    for n, ref in enumerate((tok, cot)):
        cat[0:TOK] = ref[...]
        cat[TOK : TOK + HALO] = row_in[n]
        cat[TOK + HALO : TOK + 2 * HALO] = col_in[n]
        cat[TOK + 2 * HALO : CAT] = cor_in[n]
        moved = mm(order[...], cat[...]).astype(bf16)
        if n == 0:
            keep[:, 0:D] = moved
            send[:, 0:D] = moved
        else:
            grad[...] = moved

    sub = lax.broadcasted_iota(jnp.int32, (WIN2, WIDE), 0)
    lane = lax.broadcasted_iota(jnp.int32, (WIN2, WIDE), 1) % WIN2
    row_ids, col_ids = [], []
    for i in range(SIDE):
        row_ids.append(row_field[0, lax.rem(place[0] + SHIFT + i, row_field.shape[1])] * 1024)
        col_ids.append(col_field[0, lax.rem(place[1] + SHIFT + i, col_field.shape[1])])

    def spread_ids(ids, index):
        out = jnp.zeros((WIN2, WIDE), jnp.int32)
        for i in range(WIN):
            out = jnp.where(index == i, ids[i], out)
        return out

    row_same, col_same = [], []
    for n in range(2):
        part = slice(n * WIN, (n + 1) * WIN)
        row_same.append(spread_ids(row_ids[part], sub // WIN) == spread_ids(row_ids[part], lane // WIN))
        col_same.append(spread_ids(col_ids[part], sub % WIN) == spread_ids(col_ids[part], lane % WIN))
    allowed = [(row_same[w // 2] & col_same[w % 2]).astype(f32) for w in range(WINDOWS)]
    mask = mask_ref[...]
    ones = ones_ref[...]
    head_lane = lax.broadcasted_iota(jnp.int32, (WIN2, LANES), 1) // (LANES // GROUP)
    wide_lane = lax.broadcasted_iota(jnp.int32, (1, WIDE), 1) // WIN2

    def own_heads(full):
        out = full[:WIN2]
        for h in range(1, GROUP):
            out = jnp.where(head_lane == h, full[h * WIN2 : (h + 1) * WIN2], out)
        return out

    def scale_of(g):
        out = jnp.zeros((1, WIDE), f32)
        for h in range(GROUP):
            out = jnp.where(wide_lane == h, logit_scale[g * GROUP + h], out)
        return out

    for t in range(3):
        loads[t].wait()

        @pl.loop(0, 2)
        def _(n):
            cols = pl.ds(pl.multiple_of(t * D + n * 512, 512), 512)
            qkv[:, cols] = (mm(keep[:, 0:D], wqkv[:, cols]) + bqkv[:, cols]).astype(bf16)

    loads[3].wait()

    @pl.loop(0, GROUPS)
    def _(g):
        at = pl.multiple_of(g * LANES, LANES)
        qs = pl.ds(at, LANES)
        q = qkv[:, qs].astype(f32)
        k = qkv[:, pl.ds(at + D, LANES)].astype(f32)
        v = qkv[:, pl.ds(at + 2 * D, LANES)]
        q_inv = inverse_length(q, ones)
        k_inv = inverse_length(k, ones)
        qu = (q * q_inv).astype(bf16)
        ku = (k * k_inv).astype(bf16)
        inverses[0, :, qs] = q_inv
        inverses[1, :, qs] = k_inv
        units[0, :, qs] = qu
        units[1, :, qs] = ku
        sc = scale_of(g)
        bias = bias_t[g]
        for w in range(WINDOWS):
            rows = slice(w * WIN2, (w + 1) * WIN2)
            cosine = mm_tb(ku[rows], stacked_heads(qu[rows], mask))
            weights = jnp.exp(sc * cosine + bias) * allowed[w]
            total = jnp.sum(weights, axis=0, keepdims=True)
            attention = (weights * (1.0 / total)).astype(bf16)
            att[g, w] = attention
            mixed = own_heads(mm_ta(attention, v[rows])).astype(bf16)
            keep[rows, pl.ds(at + mixed_at, LANES)] = mixed
            send[rows, pl.ds(at + mixed_at, LANES)] = mixed

    loads[4].wait()

    @pl.loop(0, 4)
    def _(n):
        cols = pl.ds(pl.multiple_of(n * 256, 256), 256)
        wide[:, cols] = mm(keep[:, mixed_at : mixed_at + D], wproj[:, cols]) + bproj[:, cols]

    gain_v = gain[...]
    shift_v = shift[...]
    vec[...] = jnp.zeros_like(vec)

    @pl.loop(0, TOK // 32)
    def _(n):
        rows = pl.ds(pl.multiple_of(n * 32, 32), 32)
        projected = wide[rows, :]
        centre = projected - jnp.mean(projected, axis=-1, keepdims=True)
        inv_std = lax.rsqrt(jnp.mean(centre * centre, axis=-1, keepdims=True) + norm_epsilon)
        normed = centre * inv_std
        branch[rows, :] = (normed * gain_v + shift_v).astype(bf16)
        go = grad[rows, :].astype(f32)
        gn = go * gain_v
        gpf = inv_std * (
            gn - jnp.mean(gn, axis=-1, keepdims=True) - normed * jnp.mean(gn * normed, axis=-1, keepdims=True)
        )
        grad[rows, :] = gpf.astype(bf16)
        vec[:, 3 * D : 4 * D] += jnp.sum(gpf, axis=0, keepdims=True)
        vec[:, 4 * D : 5 * D] += jnp.sum(go * normed, axis=0, keepdims=True)
        vec[:, 5 * D : 6 * D] += jnp.sum(go, axis=0, keepdims=True)

    put_back(order_t, branch[...], b_own, b_row, b_col, b_cor)
    half = D // 2
    keep[:, gp_at : gp_at + half] = grad[:, pl.ds(pl.multiple_of(p * half, half), half)]
    send[:, gp_at : gp_at + half] = grad[:, pl.ds(pl.multiple_of((1 - p) * half, half), half)]

    @pl.loop(0, 4)
    def _(n):
        cols = pl.ds(pl.multiple_of(n * 256, 256), 256)
        branch[:, cols] = mm_tb(grad[...], wproj[cols, :]).astype(bf16)

    @pl.loop(0, GROUPS)
    def _(g):
        at = pl.multiple_of(g * LANES, LANES)
        qs = pl.ds(at, LANES)
        v = qkv[:, pl.ds(at + 2 * D, LANES)]
        qu = units[0, :, qs]
        ku = units[1, :, qs]
        gmx = branch[:, qs]
        sc = scale_of(g)
        pos_sum = jnp.zeros((WIN2, WIDE), f32)
        sc_sum = jnp.zeros((1, WIDE), f32)
        gqu, gku, gv = [], [], []
        for w in range(WINDOWS):
            rows = slice(w * WIN2, (w + 1) * WIN2)
            q_heads = stacked_heads(qu[rows], mask)
            g_heads = stacked_heads(gmx[rows], mask)
            cosine = mm_tb(ku[rows], q_heads)
            grad_att = mm_tb(v[rows], g_heads)
            attention = att[g, w]
            gv.append(mm(attention, g_heads))
            att_f = attention.astype(f32)
            dots = jnp.sum(grad_att * att_f, axis=0, keepdims=True)
            grad_scores = att_f * (grad_att - dots)
            pos_sum = pos_sum + grad_scores
            sc_sum = sc_sum + jnp.sum(grad_scores * cosine, axis=0, keepdims=True)
            grad_cos = (sc * grad_scores).astype(bf16)
            gku.append(mm(grad_cos, q_heads))
            gqu.append(own_heads(mm_ta(grad_cos, ku[rows])))
        vec[:, pl.ds(pl.multiple_of(6 * D + g * WIDE, WIDE), WIDE)] = sc_sum
        turned = pos_sum.T
        for h in range(GROUP):
            upper = turned[h * WIN2 : h * WIN2 + 32]
            lower = turned[h * WIN2 + 32 : (h + 1) * WIN2]
            pos[pl.ds(pl.multiple_of((g * GROUP + h) * 32, 32), 32), :] = jnp.concatenate((upper, lower), axis=1)
        results = []
        for n, got in ((0, gqu), (1, gku)):
            got = jnp.concatenate(got, axis=0)
            inv = inverses[n, :, qs]
            unit = qkv[:, pl.ds(at + n * D, LANES)].astype(f32) * inv
            results.append(inv * (got - unit * segment_sums(got * unit, ones)))
        results.append(jnp.concatenate(gv, axis=0))
        for n in range(3):
            vec[:, pl.ds(at + n * D, LANES)] = jnp.sum(results[n], axis=0, keepdims=True)
        side = g // (GROUPS // 2)
        inner = pl.multiple_of((g - side * (GROUPS // 2)) * LANES, LANES)

        def put(ref):
            for n in range(3):
                ref[:, pl.ds(g_at + n * half + inner, LANES)] = results[n].astype(bf16)

        pl.when(side == p)(lambda: put(keep))
        pl.when(side != p)(lambda: put(send))

    @pl.loop(0, 64)
    def _(n):
        tile = jnp.broadcast_to(vec[:, pl.ds(pl.multiple_of(n * LANES, LANES), LANES)], (8, LANES))
        for m in range(2):
            rows = pl.ds(pl.multiple_of((n + 64 * m) * 8, 8), 8)
            small[n + 64 * m] = jnp.concatenate((pos[rows, :], tile), axis=0).astype(bf16)


def input_grad_kernel(place, keep, send, wqkv, order_t, s_own, s_row, s_col, s_cor, total):
    p = place[2]
    half = D // 2
    for t in range(3):
        for ref, side in ((keep, p), (send, 1 - p)):
            cols = pl.ds(pl.multiple_of(t * D + side * half, half), half)
            at = 2 * D + half + t * half
            term = mm_tb(ref[:, at : at + half], wqkv[:, cols])
            if t == 0 and ref is keep:
                total[...] = term
            else:
                total[...] += term
    put_back(order_t, total[...].astype(bf16), s_own, s_row, s_col, s_cor)


def weight_grad_kernel(keep, other, small, out):
    block = out.shape[0]
    peer_rows, words = small.shape
    for n in range(block // peer_rows):
        out[n * peer_rows : (n + 1) * peer_rows, 2 * D :] = small[...]
    half = D // 2
    at = pl.multiple_of(pl.program_id(0) * block, block)
    for base, first, width, to in ((0, 2 * D + half, 3 * half, 0), (D, 2 * D, half, 3 * half)):
        a = jnp.concatenate((keep[:, pl.ds(at + base, block)], other[:, pl.ds(at + base, block)]), axis=0)
        g = jnp.concatenate((keep[:, first : first + width], other[:, first : first + width]), axis=0)
        out[:, to : to + width] = mm_ta(a, g).astype(bf16)


def sum_kernel(got, qkv_out, proj_out):
    half = D // 2
    for side in range(2):
        total = jnp.sum(got[:, side, :, 0 : 4 * half].astype(f32), axis=0)
        for t in range(3):
            qkv_out[:, t * D + side * half : t * D + (side + 1) * half] = total[:, t * half : (t + 1) * half]
        proj_out[:, side * half : (side + 1) * half] = total[:, 3 * half : 4 * half]


def finish_kernel(base, own, row, col, cor, spread, out):
    border = jnp.concatenate((col[...], cor[...]), axis=0)
    moved = own[...].astype(f32) + mm(spread[...], border)
    total = base[...].astype(f32) + moved
    out[HALO:, :] = total[HALO:].astype(bf16)
    out[:HALO, :] = (total[:HALO] + row[...].astype(f32)).astype(bf16)


def sds(shape, dtype):
    return jax.ShapeDtypeStruct(shape, dtype)


VM = pl.BlockSpec(memory_space=pltpu.VMEM)
SM = pl.BlockSpec(memory_space=pltpu.SMEM)
ANY = pl.BlockSpec(memory_space=pl.ANY)


def call(kernel, outs, scratch=(), specs=None, flops=0, bytes_accessed=0):
    return pl.pallas_call(
        kernel,
        out_shape=outs,
        in_specs=specs,
        out_specs=jax.tree.map(lambda _: VM, outs),
        scratch_shapes=list(scratch),
        compiler_params=pltpu.CompilerParams(vmem_limit_bytes=VMEM_LIMIT),
        cost_estimate=pl.CostEstimate(flops=flops, bytes_accessed=bytes_accessed, transcendentals=0),
    )


def neighbour(by_row, by_col):
    rows, cols = lax.axis_size("row"), lax.axis_size("col")
    reps = lax.axis_size("rep")
    pairs = []
    for s in range(reps):
        for r in range(rows):
            for c in range(cols):
                to = (s * rows + (r + by_row) % rows) * cols + (c + by_col) % cols
                pairs.append(((s * rows + r) * cols + c, to))
    return pairs


def per_device(
    tokens, cotangent, row_field, col_field, qkv_weight, qkv_bias, logit_scale, position_bias,
    proj_weight, proj_bias, norm_gain, norm_shift,
):
    devices = lax.axis_size(AXES)
    order = jnp.asarray(window_order(), bf16)
    order_t = jnp.asarray(window_order().T, bf16)
    spread = jnp.asarray(border_spread(), bf16)
    spread_t = jnp.asarray(border_spread().T, bf16)
    mask = jnp.asarray(head_mask(), bf16)
    ones = jnp.asarray(head_sums(), bf16)
    tok = tokens[0].reshape(TOK, D)
    cot = cotangent[0].reshape(TOK, D)

    row_in, col_in, cor_in = call(
        pack_kernel, (sds((2, HALO, D), bf16), sds((2, HALO, D), bf16), sds((2, CORNER, D), bf16)), (), [VM] * 3,
        flops=10**8, bytes_accessed=2**21,
    )(tok, cot, spread_t)
    row_in = lax.ppermute(row_in, AXES, neighbour(-1, 0))
    col_in = lax.ppermute(col_in, AXES, neighbour(0, -1))
    cor_in = lax.ppermute(cor_in, AXES, neighbour(-1, -1))

    col_index = lax.axis_index("col")
    place = jnp.stack((lax.axis_index("row") * SIDE, col_index * SIDE, col_index % 2)).astype(jnp.int32)
    bias_t = position_bias.reshape(GROUPS, GROUP, WIN2, WIN2).transpose(0, 3, 1, 2).reshape(GROUPS, WIN2, WIDE)

    keep, send, b_own, b_row, b_col, b_cor, small = call(
        local_kernel,
        (
            sds((TOK, 4 * D), bf16), sds((TOK, 4 * D), bf16), sds((TOK, D), bf16), sds((HALO, D), bf16),
            sds((HALO, D), bf16), sds((CORNER, D), bf16), sds((LANES, 16, LANES), bf16),
        ),
        [
            pltpu.VMEM((D, 3 * D), bf16), pltpu.VMEM((D, D), bf16), pltpu.VMEM((GROUPS, WIN2, WIDE), f32),
            pltpu.VMEM((CAT, D), bf16), pltpu.VMEM((TOK, 3 * D), bf16),
            pltpu.VMEM((GROUPS, WINDOWS, WIN2, WIDE), bf16), pltpu.VMEM((2, TOK, D), bf16),
            pltpu.VMEM((2, TOK, D), f32), pltpu.VMEM((TOK, D), bf16), pltpu.VMEM((TOK, D), f32),
            pltpu.VMEM((TOK, D), bf16), pltpu.VMEM((HEADS * 32, LANES), f32), pltpu.VMEM((1, 8 * D), f32),
            pltpu.SemaphoreType.DMA((5,)),
        ],
        [SM] * 4 + [VM] * 9 + [ANY, VM, ANY, ANY, VM, VM, VM],
        flops=5 * 10**9, bytes_accessed=20 * 2**20,
    )(
        place, row_field, col_field, logit_scale, tok, cot, row_in, col_in, cor_in, order, order_t, mask, ones,
        qkv_weight, qkv_bias.reshape(1, -1), bias_t, proj_weight, proj_bias.reshape(1, -1),
        norm_gain.reshape(1, -1), norm_shift.reshape(1, -1),
    )
    chunks = LANES // devices
    small = lax.all_to_all(small.reshape(devices, chunks * 16, LANES), AXES, 0, 0, tiled=True)
    small = jnp.sum(small.astype(f32), axis=0).astype(bf16)

    col_size = lax.axis_size("col")
    other = lax.ppermute(send, "col", [(i, i ^ 1) for i in range(col_size)])
    s_own, s_row, s_col, s_cor = call(
        input_grad_kernel,
        (sds((TOK, D), bf16), sds((HALO, D), bf16), sds((HALO, D), bf16), sds((CORNER, D), bf16)),
        [pltpu.VMEM((TOK, D), f32)],
        [SM] + [VM] * 4,
        flops=2 * 10**9, bytes_accessed=9 * 2**20,
    )(place, keep, send, qkv_weight, order_t)

    def sent_back(row, col, cor):
        return (
            lax.ppermute(row, AXES, neighbour(1, 0)),
            lax.ppermute(col, AXES, neighbour(0, 1)),
            lax.ppermute(cor, AXES, neighbour(1, 1)),
        )

    b_got = sent_back(b_row, b_col, b_cor)
    s_got = sent_back(s_row, s_col, s_cor)

    block = 256
    rows = D // devices
    extra = 2 * LANES
    small = small.reshape(-1, 16, LANES)
    small = jnp.concatenate((small[:, :8], small[:, 8:]), axis=2).reshape(rows, extra)
    part = pl.pallas_call(
        weight_grad_kernel,
        grid=(D // block,),
        out_shape=sds((D, 2 * D + extra), bf16),
        in_specs=[pl.BlockSpec((TOK, 4 * D), lambda i: (0, 0))] * 2
        + [pl.BlockSpec((rows, extra), lambda i: (0, 0))],
        out_specs=pl.BlockSpec((block, 2 * D + extra), lambda i: (i, 0)),
        compiler_params=pltpu.CompilerParams(vmem_limit_bytes=VMEM_LIMIT),
        cost_estimate=pl.CostEstimate(flops=8 * TOK * D * D, bytes_accessed=8 * 2**20, transcendentals=0),
    )(keep, other, small)
    part, b_got, s_got = lax.optimization_barrier((part, b_got, s_got))
    got = lax.all_to_all(part.reshape(devices, rows, 2 * D + extra), AXES, 0, 0, tiled=True)
    def finish(base, own, got):
        out = call(finish_kernel, sds((TOK, D), bf16), (), [VM] * 6, flops=10**8, bytes_accessed=2**21)(
            base, own, *got, spread
        )
        return out.reshape(1, SIDE, SIDE, D)

    block_out = finish(tok, b_own, b_got)
    grad_tokens = finish(cot, s_own, s_got)

    grad_qkv_weight, grad_proj_weight = call(
        sum_kernel, (sds((rows, 3 * D), f32), sds((rows, D), f32)), (), [VM], flops=10**7, bytes_accessed=2**22
    )(got.reshape(devices // 2, 2, rows, 2 * D + extra))
    small = got[:, :, 2 * D :].reshape(LANES, 8, extra)
    grad_position = small[:, :, :LANES].reshape(HEADS, WIN2 // 2, 2, WIN2).transpose(0, 2, 1, 3)
    grad_position = grad_position.reshape(HEADS, WIN2, WIN2).astype(f32)
    vector = small[:64, 0, LANES:].astype(f32).reshape(-1)
    grad_scale = vector[6 * D :].reshape(HEADS, WIN2).sum(axis=1)
    return (
        block_out, grad_tokens, grad_qkv_weight, grad_proj_weight, vector[: 3 * D], vector[3 * D : 4 * D],
        vector[4 * D : 5 * D], vector[5 * D : 6 * D], grad_scale, grad_position,
    )


def solution(mesh):
    grid = P("rep", "row", "col", None)
    rows = P(AXES, None)
    return jax.shard_map(
        per_device,
        mesh=mesh,
        in_specs=(grid, grid, P("rep", None), P("rep", None)) + (P(),) * 8,
        out_specs=(grid, grid, rows, rows) + (P(),) * 6,
        check_vma=False,
    )
```

```python
import functools

import jax
import jax.numpy as jnp
import numpy as np
from jax import lax
from jax.experimental import pallas as pl
from jax.experimental.pallas import tpu as pltpu
from jax.sharding import PartitionSpec as P

HEADS = 32
WIN = 8
SHIFT = 4
SIDE = 16
TOK = SIDE * SIDE
D = 1024
HALO = (SIDE - SHIFT) * SHIFT
CORNER = SHIFT * SHIFT
BORDER = 2 * HALO + CORNER
CAT = TOK + BORDER
WIN2 = WIN * WIN
WINDOWS = TOK // WIN2
GROUP = 4
GROUPS = HEADS // GROUP
LANES = 128
WIDE = GROUP * WIN2
FUSED = 4
EXTRA = 2 * LANES
AXES = ("rep", "row", "col")

norm_epsilon = 1e-05
unit_floor = 1e-12
f32 = jnp.float32
bf16 = jnp.bfloat16
VMEM_LIMIT = 56 * 1024 * 1024


def window_order():
    order = np.zeros((TOK, CAT), np.float32)
    for r in range(SIDE):
        for c in range(SIDE):
            n = ((r // WIN) * 2 + c // WIN) * WIN2 + (r % WIN) * WIN + c % WIN
            rr, cc = r + SHIFT, c + SHIFT
            if rr < SIDE and cc < SIDE:
                m = rr * SIDE + cc
            elif cc < SIDE:
                m = TOK + (rr - SIDE) * (SIDE - SHIFT) + cc - SHIFT
            elif rr < SIDE:
                m = TOK + HALO + (rr - SHIFT) * SHIFT + (cc - SIDE)
            else:
                m = TOK + 2 * HALO + (rr - SIDE) * SHIFT + (cc - SIDE)
            order[n, m] = 1.0
    return order


def border_spread():
    spread = np.zeros((TOK, BORDER), np.float32)
    for r in range(SIDE):
        for c in range(SIDE):
            if r < SHIFT and c >= SHIFT:
                spread[r * SIDE + c, r * (SIDE - SHIFT) + c - SHIFT] = 1.0
            elif r >= SHIFT and c < SHIFT:
                spread[r * SIDE + c, HALO + (r - SHIFT) * SHIFT + c] = 1.0
            elif r < SHIFT and c < SHIFT:
                spread[r * SIDE + c, 2 * HALO + r * SHIFT + c] = 1.0
    return spread


def head_mask():
    rows = np.arange(WIDE)[:, None] // WIN2
    cols = np.arange(LANES)[None, :] // (LANES // GROUP)
    return (rows == cols).astype(np.float32)


def head_sums():
    heads = np.arange(2 * LANES) // (LANES // GROUP)
    return (heads[:, None] == heads[None, :]).astype(np.float32)


def mm(a, b):
    return jnp.dot(a, b, preferred_element_type=f32)


def mm_tb(a, b):
    return lax.dot_general(a, b, (((1,), (1,)), ((), ())), preferred_element_type=f32)


def mm_ta(a, b):
    return lax.dot_general(a, b, (((0,), (0,)), ((), ())), preferred_element_type=f32)


def exact_sums(values, ones):
    high = values.astype(bf16)
    low = (values - high.astype(f32)).astype(bf16)
    return mm(high, ones) + mm(low, ones)


def stacked_heads(x, mask):
    return jnp.concatenate((x, x, x, x), axis=0) * mask


def split_border(border, n, row, col, cor):
    row[n] = border[:HALO]
    col[n] = border[HALO : 2 * HALO]
    cor[n] = border[2 * HALO :]


def pack_kernel(tok, cot, spread_t, row, col, cor):
    for n, ref in enumerate((tok, cot)):
        split_border(mm(spread_t[...], ref[...]).astype(bf16), n, row, col, cor)


def local_kernel(
    place, row_field, col_field, logit_scale, tok, cot, row_in, col_in, cor_in, order, order_t, mask_ref, ones_ref,
    wqkv_hbm, bqkv, bias_hbm, wproj_hbm, bproj, gain, shift,
    send, keep, own, row, col, cor, small,
    wqkv, wproj, bias_t, cat, qkv, att, cos, units, inverses, grad, wide, branch, pos, vec,
    x, mixed, gp_send, gp_keep, g_send, g_keep, border, sems, out_sems,
):
    loads = [
        pltpu.make_async_copy(wqkv_hbm.at[:, pl.ds(t * D, D)], wqkv.at[:, pl.ds(t * D, D)], sems.at[t])
        for t in range(3)
    ]
    loads.append(pltpu.make_async_copy(bias_hbm, bias_t, sems.at[3]))
    loads.append(pltpu.make_async_copy(wproj_hbm, wproj, sems.at[4]))
    for load in loads:
        load.start()

    p = place[2]
    half = D // 2
    stores = []

    def write(source, target):
        copy = pltpu.make_async_copy(source, target, out_sems.at[len(stores)])
        copy.start()
        stores.append(copy)

    for n, ref in enumerate((tok, cot)):
        cat[0:TOK] = ref[...]
        cat[TOK : TOK + HALO] = row_in[n]
        cat[TOK + HALO : TOK + 2 * HALO] = col_in[n]
        cat[TOK + 2 * HALO : CAT] = cor_in[n]
        moved = mm(order[...], cat[...]).astype(bf16)
        if n == 0:
            x[...] = moved
            write(x, send.at[:, pl.ds(3 * half, D)])
        else:
            grad[...] = moved

    sub = lax.broadcasted_iota(jnp.int32, (WIN2, WIDE), 0)
    lane = lax.broadcasted_iota(jnp.int32, (WIN2, WIDE), 1) % WIN2
    row_ids, col_ids = [], []
    for i in range(SIDE):
        row_ids.append(row_field[0, lax.rem(place[0] + SHIFT + i, row_field.shape[1])] * 1024)
        col_ids.append(col_field[0, lax.rem(place[1] + SHIFT + i, col_field.shape[1])])

    def spread_ids(ids, index):
        out = jnp.zeros((WIN2, WIDE), jnp.int32)
        for i in range(WIN):
            out = jnp.where(index == i, ids[i], out)
        return out

    row_same, col_same = [], []
    for n in range(2):
        part = slice(n * WIN, (n + 1) * WIN)
        row_same.append(spread_ids(row_ids[part], sub // WIN) == spread_ids(row_ids[part], lane // WIN))
        col_same.append(spread_ids(col_ids[part], sub % WIN) == spread_ids(col_ids[part], lane % WIN))
    allowed = [(row_same[w // 2] & col_same[w % 2]).astype(f32) for w in range(WINDOWS)]
    mask = mask_ref[...]
    mask_pair = jnp.concatenate((mask, mask), axis=1)
    ones = ones_ref[...]
    wide_lane = lax.broadcasted_iota(jnp.int32, (1, WIDE), 1) // WIN2

    odd_head = lax.broadcasted_iota(jnp.int32, (WIN2, LANES), 1) // (LANES // GROUP) % 2 == 1

    def own_heads(full, dtype):
        picked = jnp.concatenate((full[:WIN2, :LANES], full[WIN2:, LANES:]), axis=0).astype(dtype).T
        return jnp.where(odd_head, picked[WIN2:], picked[:WIN2])

    head_lane = lax.broadcasted_iota(jnp.int32, (WIN2, LANES), 1) // (LANES // GROUP)

    def pick_heads(full):
        out = full[:WIN2]
        for h in range(1, GROUP):
            out = jnp.where(head_lane == h, full[h * WIN2 : (h + 1) * WIN2], out)
        return out

    def scale_of(g):
        out = jnp.zeros((1, WIDE), f32)
        for h in range(GROUP):
            out = jnp.where(wide_lane == h, logit_scale[g * GROUP + h], out)
        return out

    for t in range(3):
        loads[t].wait()

        @pl.loop(0, 2)
        def _(n):
            cols = pl.ds(pl.multiple_of(t * D + n * 512, 512), 512)
            qkv[:, cols] = (mm(x[...], wqkv[:, cols]) + bqkv[:, cols]).astype(bf16)

    loads[3].wait()

    def attend(g):
        at = pl.multiple_of(g * LANES, LANES)
        qs = pl.ds(at, LANES)
        q = qkv[:, qs].astype(f32)
        k = qkv[:, pl.ds(at + D, LANES)].astype(f32)
        v = qkv[:, pl.ds(at + 2 * D, LANES)]
        sc = scale_of(g)
        bias = bias_t[g]
        raw = jnp.concatenate((q, k), axis=1)
        inv = lax.rsqrt(jnp.maximum(exact_sums(raw * raw, ones), unit_floor * unit_floor))
        unit = (raw * inv).astype(bf16)
        q_inv, k_inv, qu, ku = inv[:, :LANES], inv[:, LANES:], unit[:, :LANES], unit[:, LANES:]
        cosines, attentions, mixed_parts = [], [], []
        for w in range(WINDOWS):
            rows = slice(w * WIN2, (w + 1) * WIN2)
            cosine = mm_tb(ku[rows], stacked_heads(qu[rows], mask))
            weights = jnp.exp(sc * cosine + bias) * allowed[w]
            total = jnp.sum(weights, axis=0, keepdims=True)
            attention = (weights * (1.0 / total)).astype(bf16)
            cosines.append(cosine)
            attentions.append(attention)
            mixed_parts.append(pick_heads(mm_ta(attention, v[rows])).astype(bf16))

        def store():
            inverses[0, :, qs] = q_inv
            inverses[1, :, qs] = k_inv
            units[0, :, qs] = qu
            units[1, :, qs] = ku
            for w in range(WINDOWS):
                att[g, w] = attentions[w]
                cos[g, w] = cosines[w]
            mixed[:, qs] = jnp.concatenate(mixed_parts, axis=0)

        return store

    @pl.loop(0, GROUPS // FUSED)
    def _(n):
        for store in [attend(n * FUSED + u) for u in range(FUSED)]:
            store()

    write(mixed, send.at[:, pl.ds(0, D)])
    loads[4].wait()

    @pl.loop(0, 4)
    def _(n):
        cols = pl.ds(pl.multiple_of(n * 256, 256), 256)
        wide[:, cols] = mm(mixed[...], wproj[:, cols]) + bproj[:, cols]

    gain_v = gain[...]
    shift_v = shift[...]
    vec[...] = jnp.zeros_like(vec)

    @pl.loop(0, TOK // 32)
    def _(n):
        rows = pl.ds(pl.multiple_of(n * 32, 32), 32)
        projected = wide[rows, :]
        centre = projected - jnp.mean(projected, axis=-1, keepdims=True)
        inv_std = lax.rsqrt(jnp.mean(centre * centre, axis=-1, keepdims=True) + norm_epsilon)
        normed = centre * inv_std
        branch[rows, :] = (normed * gain_v + shift_v).astype(bf16)
        go = grad[rows, :].astype(f32)
        gn = go * gain_v
        gpf = inv_std * (
            gn - jnp.mean(gn, axis=-1, keepdims=True) - normed * jnp.mean(gn * normed, axis=-1, keepdims=True)
        )
        grad[rows, :] = gpf.astype(bf16)
        vec[:, 3 * D : 4 * D] += jnp.sum(gpf, axis=0, keepdims=True)
        vec[:, 4 * D : 5 * D] += jnp.sum(go * normed, axis=0, keepdims=True)
        vec[:, 5 * D : 6 * D] += jnp.sum(go, axis=0, keepdims=True)

    gp_keep[...] = grad[:, pl.ds(pl.multiple_of(p * half, half), half)]
    gp_send[...] = grad[:, pl.ds(pl.multiple_of((1 - p) * half, half), half)]
    write(gp_keep, keep.at[:, pl.ds(0, half)])
    write(gp_send, send.at[:, pl.ds(D, half)])

    def give_back(n, values):
        border[n] = mm(order_t[...], values).astype(bf16)
        first = 0
        for ref, count in ((own, TOK), (row, HALO), (col, HALO), (cor, CORNER)):
            write(border.at[n, pl.ds(first, count), :], ref.at[n])
            first += count

    give_back(0, branch[...])

    @pl.loop(0, 4)
    def _(n):
        cols = pl.ds(pl.multiple_of(n * 256, 256), 256)
        branch[:, cols] = mm_tb(grad[...], wproj[cols, :]).astype(bf16)

    def attend_back(g):
        at = pl.multiple_of(g * LANES, LANES)
        qs = pl.ds(at, LANES)
        v = qkv[:, pl.ds(at + 2 * D, LANES)]
        qu = units[0, :, qs]
        ku = units[1, :, qs]
        gmx = branch[:, qs]
        sc = scale_of(g)
        attentions = [att[g, w] for w in range(WINDOWS)]
        cosines = [cos[g, w] for w in range(WINDOWS)]
        invs = [inverses[n, :, qs] for n in range(2)]
        raws = [qkv[:, pl.ds(at + n * D, LANES)] for n in range(2)]
        pos_sum = jnp.zeros((WIN2, WIDE), f32)
        sc_sum = jnp.zeros((WIN2, WIDE), f32)
        gqu, gku, gv = [], [], []
        for w in range(WINDOWS):
            rows = slice(w * WIN2, (w + 1) * WIN2)
            both = stacked_heads(jnp.concatenate((gmx[rows], qu[rows]), axis=1), mask_pair)
            grad_att = mm_tb(v[rows], both[:, :LANES])
            attention = attentions[w]
            att_f = attention.astype(f32)
            dots = jnp.sum(grad_att * att_f, axis=0, keepdims=True)
            grad_scores = att_f * (grad_att - dots)
            pos_sum = pos_sum + grad_scores
            sc_sum = sc_sum + grad_scores * cosines[w]
            grad_cos = (sc * grad_scores).astype(bf16)
            pair = mm(jnp.concatenate((attention, grad_cos), axis=0), both)
            gv.append(pair[:WIN2, :LANES])
            gku.append(pair[WIN2:, LANES:])
            gqu.append(own_heads(mm_ta(ku[rows], grad_cos), f32))
        turned = pos_sum.T
        pos_parts = []
        for h in range(GROUP):
            upper = turned[h * WIN2 : h * WIN2 + 32]
            lower = turned[h * WIN2 + 32 : (h + 1) * WIN2]
            pos_parts.append(jnp.concatenate((upper, lower), axis=1))
        got = jnp.concatenate((jnp.concatenate(gqu, axis=0), jnp.concatenate(gku, axis=0)), axis=1)
        inv = jnp.concatenate(invs, axis=1)
        unit = jnp.concatenate(raws, axis=1).astype(f32) * inv
        got = inv * (got - unit * mm((got * unit).astype(bf16), ones))
        results = [got[:, :LANES], got[:, LANES:]]
        results.append(jnp.concatenate(gv, axis=0))
        sums = [jnp.sum(result, axis=0, keepdims=True) for result in results]
        sc_row = jnp.sum(sc_sum, axis=0, keepdims=True)
        inner = pl.multiple_of(lax.rem(g, GROUPS // 2) * LANES, LANES)

        def store():
            vec[:, pl.ds(pl.multiple_of(6 * D + g * WIDE, WIDE), WIDE)] = sc_row
            pos[pl.ds(pl.multiple_of(g * LANES, LANES), LANES), :] = jnp.concatenate(pos_parts, axis=0)
            for n in range(3):
                vec[:, pl.ds(at + n * D, LANES)] = sums[n]

            def put(ref):
                for n in range(3):
                    ref[:, pl.ds(n * half + inner, LANES)] = results[n].astype(bf16)

            side = g // (GROUPS // 2)
            pl.when(side == p)(lambda: put(g_keep))
            pl.when(side != p)(lambda: put(g_send))

        return store

    @pl.loop(0, GROUPS // FUSED)
    def _(n):
        for store in [attend_back(n * FUSED + u) for u in range(FUSED)]:
            store()

    write(g_keep, keep.at[:, pl.ds(half, 3 * half)])
    write(g_send, send.at[:, pl.ds(5 * half, 3 * half)])

    @pl.loop(0, 64)
    def _(n):
        rows = pl.ds(pl.multiple_of(n * 16, 16), 16)
        tiles = []
        for m in range(2):
            at = pl.multiple_of(lax.rem(2 * n + m, 64) * LANES, LANES)
            tiles.append(jnp.broadcast_to(vec[:, pl.ds(at, LANES)], (8, LANES)))
        small[rows, :] = jnp.concatenate((pos[rows, :], jnp.concatenate(tiles, axis=0)), axis=1).astype(bf16)

    @pl.loop(0, 4)
    def _(n):
        rows = pl.ds(pl.multiple_of(n * 256, 256), 256)
        total = jnp.zeros((TOK, 256), f32)
        for t in range(3):
            for ref, side in ((g_keep, p), (g_send, 1 - p)):
                cols = pl.ds(pl.multiple_of(t * D + side * half, half), half)
                total = total + mm_tb(ref[:, t * half : (t + 1) * half], wqkv[rows, cols])
        branch[:, rows] = total.astype(bf16)

    give_back(1, branch[...])
    for copy in stores:
        copy.wait()


def weight_grad_kernel(mixed, x, mixed_other, x_other, keep, gp_other, q_other, k_other, v_other, out):
    half = D // 2
    a = jnp.concatenate((x[...], x_other[...]), axis=0)
    for t, ref in enumerate((q_other, k_other, v_other)):
        g = jnp.concatenate((keep[:, (t + 1) * half : (t + 2) * half], ref[...]), axis=0)
        out[:, t * half : (t + 1) * half] = mm_ta(a, g).astype(bf16)
    a = jnp.concatenate((mixed[...], mixed_other[...]), axis=0)
    g = jnp.concatenate((keep[:, 0:half], gp_other[...]), axis=0)
    out[:, 3 * half : 4 * half] = mm_ta(a, g).astype(bf16)


def fold_kernel(got, part, part_out, spread_small, sem):
    devices, rows, _ = got.shape
    small = jnp.sum(got[...].astype(f32), axis=0)
    spread_small[...] = jnp.broadcast_to(small[None], (devices, rows, EXTRA)).reshape(D, EXTRA).astype(bf16)
    copy = pltpu.make_async_copy(spread_small, part_out.at[:, pl.ds(2 * D, EXTRA)], sem)
    copy.start()
    copy.wait()


def last_kernel(got, qkv_out, proj_out, pos_out, qkv_bias, proj_bias, gain, shift, scale, total, small):
    half = D // 2
    step = pl.program_id(0)
    pairs, _, rows, _ = got.shape
    count = 2 * pairs * rows

    @pl.when(step == 0)
    def _():
        total[...] = jnp.zeros_like(total)

    for side in range(2):
        total[side] += jnp.sum(got[:, side, :, 0 : 4 * half].astype(f32), axis=0)
    here = got[:, :, :, 4 * half :].astype(f32).reshape(count, EXTRA)
    small[pl.ds(pl.multiple_of(step * count, count), count), :] = here

    @pl.when(step == pl.num_programs(0) - 1)
    def _():
        for side in range(2):
            for t in range(3):
                first = t * D + side * half
                qkv_out[:, first : first + half] = total[side, :, t * half : (t + 1) * half]
            proj_out[:, side * half : (side + 1) * half] = total[side, :, 3 * half :]
        folded = small[:, 0:LANES].reshape(HEADS, WIN2 // 2, LANES)
        pos_out[:, 0 : WIN2 // 2, :] = folded[:, :, 0:WIN2]
        pos_out[:, WIN2 // 2 :, :] = folded[:, :, WIN2:]
        first = 0
        for ref in (qkv_bias, proj_bias, gain, shift):
            for n in range(ref.shape[0] // LANES):
                ref[n * LANES : (n + 1) * LANES] = small[8 * (first + n), LANES:]
            first += ref.shape[0] // LANES
        lane = lax.broadcasted_iota(jnp.int32, (1, LANES), 1)
        heads = jnp.zeros((1, LANES), f32)
        for n in range(HEADS // 2):
            pair = small[8 * (first + n) : 8 * (first + n) + 1, LANES:]
            heads = jnp.where(lane == 2 * n, jnp.sum(pair[:, :WIN2], axis=1, keepdims=True), heads)
            heads = jnp.where(lane == 2 * n + 1, jnp.sum(pair[:, WIN2:], axis=1, keepdims=True), heads)
        scale[...] = heads[0, :HEADS]


def finish_kernel(tok, cot, own, row, col, cor, spread, block_out, grad_tokens):
    for n, (base, out) in enumerate(((tok, block_out), (cot, grad_tokens))):
        border = jnp.concatenate((row[n], col[n], cor[n]), axis=0)
        moved = own[n].astype(f32) + mm(spread[...], border)
        out[...] = (base[...].astype(f32) + moved).astype(bf16)


def sds(shape, dtype):
    return jax.ShapeDtypeStruct(shape, dtype)


VM = pl.BlockSpec(memory_space=pltpu.VMEM)
SM = pl.BlockSpec(memory_space=pltpu.SMEM)
ANY = pl.BlockSpec(memory_space=pl.ANY)


def call(kernel, outs, scratch=(), specs=None, flops=0, bytes_accessed=0, out_specs=None):
    return pl.pallas_call(
        kernel,
        out_shape=outs,
        in_specs=specs,
        out_specs=out_specs or jax.tree.map(lambda _: VM, outs),
        scratch_shapes=list(scratch),
        compiler_params=pltpu.CompilerParams(vmem_limit_bytes=VMEM_LIMIT),
        cost_estimate=pl.CostEstimate(flops=flops, bytes_accessed=bytes_accessed, transcendentals=0),
    )


def neighbour(by_row, by_col):
    rows, cols = lax.axis_size("row"), lax.axis_size("col")
    reps = lax.axis_size("rep")
    pairs = []
    for s in range(reps):
        for r in range(rows):
            for c in range(cols):
                to = (s * rows + (r + by_row) % rows) * cols + (c + by_col) % cols
                pairs.append(((s * rows + r) * cols + c, to))
    return pairs


def per_device(
    tokens, cotangent, row_field, col_field, qkv_weight, qkv_bias, logit_scale, position_bias,
    proj_weight, proj_bias, norm_gain, norm_shift,
):
    devices = lax.axis_size(AXES)
    order = jnp.asarray(window_order(), bf16)
    order_t = jnp.asarray(window_order().T, bf16)
    spread = jnp.asarray(border_spread(), bf16)
    spread_t = jnp.asarray(border_spread().T, bf16)
    mask = jnp.asarray(head_mask(), bf16)
    ones = jnp.asarray(head_sums(), bf16)
    tok = tokens[0].reshape(TOK, D)
    cot = cotangent[0].reshape(TOK, D)

    row_in, col_in, cor_in = call(
        pack_kernel, (sds((2, HALO, D), bf16), sds((2, HALO, D), bf16), sds((2, CORNER, D), bf16)), (), [VM] * 3,
        flops=10**8, bytes_accessed=2**21,
    )(tok, cot, spread_t)
    row_in = lax.ppermute(row_in, AXES, neighbour(-1, 0))
    col_in = lax.ppermute(col_in, AXES, neighbour(0, -1))
    cor_in = lax.ppermute(cor_in, AXES, neighbour(-1, -1))

    col_index = lax.axis_index("col")
    place = jnp.stack((lax.axis_index("row") * SIDE, col_index * SIDE, col_index % 2)).astype(jnp.int32)
    bias_t = position_bias.reshape(GROUPS, GROUP, WIN2, WIN2).transpose(0, 3, 1, 2).reshape(GROUPS, WIN2, WIDE)

    send, keep, own, row, col, cor, small = call(
        local_kernel,
        (
            sds((TOK, 4 * D), bf16), sds((TOK, 2 * D), bf16),
            sds((2, TOK, D), bf16), sds((2, HALO, D), bf16), sds((2, HALO, D), bf16), sds((2, CORNER, D), bf16),
            sds((D, EXTRA), bf16),
        ),
        [
            pltpu.VMEM((D, 3 * D), bf16), pltpu.VMEM((D, D), bf16), pltpu.VMEM((GROUPS, WIN2, WIDE), f32),
            pltpu.VMEM((CAT, D), bf16), pltpu.VMEM((TOK, 3 * D), bf16),
            pltpu.VMEM((GROUPS, WINDOWS, WIN2, WIDE), bf16), pltpu.VMEM((GROUPS, WINDOWS, WIN2, WIDE), f32),
            pltpu.VMEM((2, TOK, D), bf16), pltpu.VMEM((2, TOK, D), f32), pltpu.VMEM((TOK, D), bf16),
            pltpu.VMEM((TOK, D), f32), pltpu.VMEM((TOK, D), bf16), pltpu.VMEM((HEADS * 32, LANES), f32),
            pltpu.VMEM((1, 8 * D), f32), pltpu.VMEM((TOK, D), bf16), pltpu.VMEM((TOK, D), bf16),
            pltpu.VMEM((TOK, D // 2), bf16), pltpu.VMEM((TOK, D // 2), bf16), pltpu.VMEM((TOK, 3 * D // 2), bf16),
            pltpu.VMEM((TOK, 3 * D // 2), bf16), pltpu.VMEM((2, CAT, D), bf16),
            pltpu.SemaphoreType.DMA((5,)), pltpu.SemaphoreType.DMA((14,)),
        ],
        [SM] * 4 + [VM] * 9 + [ANY, VM, ANY, ANY, VM, VM, VM],
        flops=5 * 10**9, bytes_accessed=20 * 2**20, out_specs=(ANY,) * 6 + (VM,),
    )(
        place, row_field, col_field, logit_scale, tok, cot, row_in, col_in, cor_in, order, order_t, mask, ones,
        qkv_weight, qkv_bias.reshape(1, -1), bias_t, proj_weight, proj_bias.reshape(1, -1),
        norm_gain.reshape(1, -1), norm_shift.reshape(1, -1),
    )
    col_size = lax.axis_size("col")
    cores = [(i, i ^ 1) for i in range(col_size)]
    other = lax.ppermute(send, "col", cores)
    rows = D // devices
    small = lax.all_to_all(small.reshape(devices, rows, EXTRA), AXES, 0, 0, tiled=True)
    row = lax.ppermute(row, AXES, neighbour(1, 0))
    col = lax.ppermute(col, AXES, neighbour(0, 1))
    cor = lax.ppermute(cor, AXES, neighbour(1, 1))
    block = D // 2

    def columns(first, moving):
        return pl.BlockSpec((TOK, block), lambda i: (0, first + (i if moving else 0)))

    part = pl.pallas_call(
        weight_grad_kernel,
        grid=(2,),
        out_shape=sds((D, 2 * D + EXTRA), bf16),
        in_specs=[
            columns(0, True), columns(3, True), columns(0, True), columns(3, True),
            pl.BlockSpec((TOK, 2 * D), lambda i: (0, 0)),
            columns(2, False), columns(5, False), columns(6, False), columns(7, False),
        ],
        out_specs=pl.BlockSpec((block, 2 * D + EXTRA), lambda i: (i, 0)),
        compiler_params=pltpu.CompilerParams(vmem_limit_bytes=VMEM_LIMIT),
        cost_estimate=pl.CostEstimate(flops=8 * TOK * D * D, bytes_accessed=8 * 2**20, transcendentals=0),
    )(send, send, other, other, keep, other, other, other, other)
    part, small = lax.optimization_barrier((part, small))
    part = pl.pallas_call(
        fold_kernel,
        out_shape=sds(part.shape, bf16),
        in_specs=[VM, ANY],
        out_specs=ANY,
        scratch_shapes=[pltpu.VMEM((D, EXTRA), bf16), pltpu.SemaphoreType.DMA],
        input_output_aliases={1: 0},
        compiler_params=pltpu.CompilerParams(vmem_limit_bytes=VMEM_LIMIT),
        cost_estimate=pl.CostEstimate(flops=10**6, bytes_accessed=2**20, transcendentals=0),
    )(small, part)
    part, row, col, cor = lax.optimization_barrier((part, row, col, cor))
    got = lax.all_to_all(part.reshape(devices, rows, -1), AXES, 0, 0, tiled=True)
    block_out, grad_tokens = call(
        finish_kernel, (sds((TOK, D), bf16), sds((TOK, D), bf16)), (), [VM] * 7, flops=10**8, bytes_accessed=2**22
    )(tok, cot, own, row, col, cor, spread)
    steps = 4
    outs = (
        sds((rows, 3 * D), f32), sds((rows, D), f32), sds((HEADS, WIN2, WIN2), f32), sds((3 * D,), f32), sds((D,), f32),
        sds((D,), f32), sds((D,), f32), sds((HEADS,), f32),
    )
    grad_qkv_weight, grad_proj_weight, grad_position, g_qkv_bias, g_proj_bias, g_gain, g_shift, g_scale = pl.pallas_call(
        last_kernel,
        grid=(steps,),
        out_shape=outs,
        in_specs=[pl.BlockSpec((devices // 2 // steps, 2, rows, got.shape[2]), lambda i: (i, 0, 0, 0))],
        out_specs=tuple(pl.BlockSpec(o.shape, lambda i, n=len(o.shape): (0,) * n) for o in outs),
        scratch_shapes=[pltpu.VMEM((2, rows, 2 * D), f32), pltpu.VMEM((D, EXTRA), f32)],
        compiler_params=pltpu.CompilerParams(vmem_limit_bytes=VMEM_LIMIT),
        cost_estimate=pl.CostEstimate(flops=10**7, bytes_accessed=2**22, transcendentals=0),
    )(got.reshape(devices // 2, 2, rows, -1))
    return (
        block_out.reshape(1, SIDE, SIDE, D), grad_tokens.reshape(1, SIDE, SIDE, D), grad_qkv_weight, grad_proj_weight, g_qkv_bias, g_proj_bias,
        g_gain, g_shift, g_scale, grad_position,
    )


def solution(mesh):
    grid = P("rep", "row", "col", None)
    rows = P(AXES, None)
    return jax.shard_map(
        per_device,
        mesh=mesh,
        in_specs=(grid, grid, P("rep", None), P("rep", None)) + (P(),) * 8,
        out_specs=(grid, grid, rows, rows) + (P(),) * 6,
        check_vma=False,
    )
```

```python
import functools

import jax
import jax.numpy as jnp
import numpy as np
from jax import lax
from jax.experimental import pallas as pl
from jax.experimental.pallas import tpu as pltpu
from jax.sharding import PartitionSpec as P

HEADS = 32
WIN = 8
SHIFT = 4
SIDE = 16
TOK = SIDE * SIDE
D = 1024
HALO = (SIDE - SHIFT) * SHIFT
CORNER = SHIFT * SHIFT
BORDER = 2 * HALO + CORNER
CAT = TOK + BORDER
WIN2 = WIN * WIN
WINDOWS = TOK // WIN2
GROUP = 4
GROUPS = HEADS // GROUP
LANES = 128
WIDE = GROUP * WIN2
FUSED = 8
EXTRA = 2 * LANES
AXES = ("rep", "row", "col")

norm_epsilon = 1e-05
unit_floor = 1e-12
f32 = jnp.float32
bf16 = jnp.bfloat16
VMEM_LIMIT = 56 * 1024 * 1024


def window_order():
    order = np.zeros((TOK, CAT), np.float32)
    for r in range(SIDE):
        for c in range(SIDE):
            n = ((r // WIN) * 2 + c // WIN) * WIN2 + (r % WIN) * WIN + c % WIN
            rr, cc = r + SHIFT, c + SHIFT
            if rr < SIDE and cc < SIDE:
                m = rr * SIDE + cc
            elif cc < SIDE:
                m = TOK + (rr - SIDE) * (SIDE - SHIFT) + cc - SHIFT
            elif rr < SIDE:
                m = TOK + HALO + (rr - SHIFT) * SHIFT + (cc - SIDE)
            else:
                m = TOK + 2 * HALO + (rr - SIDE) * SHIFT + (cc - SIDE)
            order[n, m] = 1.0
    return order


def border_spread():
    spread = np.zeros((TOK, BORDER), np.float32)
    for r in range(SIDE):
        for c in range(SIDE):
            if r < SHIFT and c >= SHIFT:
                spread[r * SIDE + c, r * (SIDE - SHIFT) + c - SHIFT] = 1.0
            elif r >= SHIFT and c < SHIFT:
                spread[r * SIDE + c, HALO + (r - SHIFT) * SHIFT + c] = 1.0
            elif r < SHIFT and c < SHIFT:
                spread[r * SIDE + c, 2 * HALO + r * SHIFT + c] = 1.0
    return spread


def head_mask():
    rows = np.arange(WIDE)[:, None] // WIN2
    cols = np.arange(LANES)[None, :] // (LANES // GROUP)
    return (rows == cols).astype(np.float32)


def head_sums():
    heads = np.arange(2 * LANES) // (LANES // GROUP)
    return (heads[:, None] == heads[None, :]).astype(np.float32)


def mm(a, b):
    return jnp.dot(a, b, preferred_element_type=f32)


def mm_tb(a, b):
    return lax.dot_general(a, b, (((1,), (1,)), ((), ())), preferred_element_type=f32)


def mm_ta(a, b):
    return lax.dot_general(a, b, (((0,), (0,)), ((), ())), preferred_element_type=f32)


def exact_sums(values, ones):
    high = values.astype(bf16)
    low = (values - high.astype(f32)).astype(bf16)
    return mm(high, ones) + mm(low, ones)


def stacked_heads(x, mask):
    return jnp.concatenate((x, x, x, x), axis=0) * mask


def in_step(parts):
    while parts:
        parts = [part for part in parts if next(part, parts) is not parts]


def split_border(border, n, row, col, cor):
    row[n] = border[:HALO]
    col[n] = border[HALO : 2 * HALO]
    cor[n] = border[2 * HALO :]


def pack_kernel(tok, cot, spread_t, row, col, cor):
    for n, ref in enumerate((tok, cot)):
        split_border(mm(spread_t[...], ref[...]).astype(bf16), n, row, col, cor)


def local_kernel(
    place, row_field, col_field, logit_scale, tok, cot, row_in, col_in, cor_in, order, order_t, mask_ref, ones_ref,
    wqkv_hbm, bqkv, bias_hbm, wproj_hbm, bproj, gain, shift,
    send, keep, own, row, col, cor, small,
    wqkv, wproj, bias_t, cat, qkv, att, cos, units, inverses, grad, wide, branch, pos, vec,
    x, mixed, gp_send, gp_keep, g_send, g_keep, border, sems, out_sems,
):
    loads = [
        pltpu.make_async_copy(wqkv_hbm.at[:, pl.ds(t * D, D)], wqkv.at[:, pl.ds(t * D, D)], sems.at[t])
        for t in range(3)
    ]
    loads.append(pltpu.make_async_copy(bias_hbm, bias_t, sems.at[3]))
    loads.append(pltpu.make_async_copy(wproj_hbm, wproj, sems.at[4]))
    for load in loads:
        load.start()

    p = place[2]
    half = D // 2
    stores = []

    def write(source, target):
        copy = pltpu.make_async_copy(source, target, out_sems.at[len(stores)])
        copy.start()
        stores.append(copy)

    for n, ref in enumerate((tok, cot)):
        cat[0:TOK] = ref[...]
        cat[TOK : TOK + HALO] = row_in[n]
        cat[TOK + HALO : TOK + 2 * HALO] = col_in[n]
        cat[TOK + 2 * HALO : CAT] = cor_in[n]
        moved = mm(order[...], cat[...]).astype(bf16)
        if n == 0:
            x[...] = moved
            write(x, send.at[:, pl.ds(3 * half, D)])
        else:
            grad[...] = moved

    sub = lax.broadcasted_iota(jnp.int32, (WIN2, WIDE), 0)
    lane = lax.broadcasted_iota(jnp.int32, (WIN2, WIDE), 1) % WIN2
    row_ids, col_ids = [], []
    for i in range(SIDE):
        row_ids.append(row_field[0, lax.rem(place[0] + SHIFT + i, row_field.shape[1])] * 1024)
        col_ids.append(col_field[0, lax.rem(place[1] + SHIFT + i, col_field.shape[1])])

    def spread_ids(ids, index):
        out = jnp.zeros((WIN2, WIDE), jnp.int32)
        for i in range(WIN):
            out = jnp.where(index == i, ids[i], out)
        return out

    row_same, col_same = [], []
    for n in range(2):
        part = slice(n * WIN, (n + 1) * WIN)
        row_same.append(spread_ids(row_ids[part], sub // WIN) == spread_ids(row_ids[part], lane // WIN))
        col_same.append(spread_ids(col_ids[part], sub % WIN) == spread_ids(col_ids[part], lane % WIN))
    allowed = [(row_same[w // 2] & col_same[w % 2]).astype(f32) for w in range(WINDOWS)]
    mask = mask_ref[...]
    mask_pair = jnp.concatenate((mask, mask), axis=1)
    ones = ones_ref[...]
    wide_lane = lax.broadcasted_iota(jnp.int32, (1, WIDE), 1) // WIN2

    odd_head = lax.broadcasted_iota(jnp.int32, (WIN2, LANES), 1) // (LANES // GROUP) % 2 == 1

    def own_heads(full, dtype):
        picked = jnp.concatenate((full[:WIN2, :LANES], full[WIN2:, LANES:]), axis=0).astype(dtype).T
        return jnp.where(odd_head, picked[WIN2:], picked[:WIN2])

    head_lane = lax.broadcasted_iota(jnp.int32, (WIN2, LANES), 1) // (LANES // GROUP)

    def pick_heads(full):
        out = full[:WIN2]
        for h in range(1, GROUP):
            out = jnp.where(head_lane == h, full[h * WIN2 : (h + 1) * WIN2], out)
        return out

    window_rows = [slice(w * WIN2, (w + 1) * WIN2) for w in range(WINDOWS)]

    def scale_of(g):
        out = jnp.zeros((1, WIDE), f32)
        for h in range(GROUP):
            out = jnp.where(wide_lane == h, logit_scale[g * GROUP + h], out)
        return out

    for t in range(3):
        loads[t].wait()

        @pl.loop(0, 2)
        def _(n):
            cols = pl.ds(pl.multiple_of(t * D + n * 512, 512), 512)
            qkv[:, cols] = (mm(x[...], wqkv[:, cols]) + bqkv[:, cols]).astype(bf16)

    loads[3].wait()

    def attend(g):
        at = pl.multiple_of(g * LANES, LANES)
        qs = pl.ds(at, LANES)
        v = qkv[:, pl.ds(at + 2 * D, LANES)]
        raw = jnp.concatenate((qkv[:, qs], qkv[:, pl.ds(at + D, LANES)]), axis=1).astype(f32)
        total = exact_sums(raw * raw, ones)
        yield
        inv = lax.rsqrt(jnp.maximum(total, unit_floor * unit_floor))
        unit = (raw * inv).astype(bf16)
        qu, ku = unit[:, :LANES], unit[:, LANES:]
        cosines = [mm_tb(ku[rows], stacked_heads(qu[rows], mask)) for rows in window_rows]
        yield
        sc = scale_of(g)
        bias = bias_t[g]
        attentions = []
        for w in range(WINDOWS):
            weights = jnp.exp(sc * cosines[w] + bias) * allowed[w]
            total = jnp.sum(weights, axis=0, keepdims=True)
            attentions.append((weights * (1.0 / total)).astype(bf16))
        products = [mm_ta(attentions[w], v[window_rows[w]]) for w in range(WINDOWS)]
        yield
        for n in range(2):
            inverses[n, :, qs] = inv[:, n * LANES : (n + 1) * LANES]
            units[n, :, qs] = unit[:, n * LANES : (n + 1) * LANES]
        for w in range(WINDOWS):
            att[g, w] = attentions[w]
            cos[g, w] = cosines[w]
        mixed[:, qs] = jnp.concatenate([pick_heads(product).astype(bf16) for product in products], axis=0)

    @pl.loop(0, GROUPS // FUSED)
    def _(n):
        in_step([attend(n * FUSED + u) for u in range(FUSED)])

    write(mixed, send.at[:, pl.ds(0, D)])
    loads[4].wait()

    @pl.loop(0, 4)
    def _(n):
        cols = pl.ds(pl.multiple_of(n * 256, 256), 256)
        wide[:, cols] = mm(mixed[...], wproj[:, cols]) + bproj[:, cols]

    gain_v = gain[...]
    shift_v = shift[...]

    projected = wide[...]
    centre = projected - jnp.mean(projected, axis=-1, keepdims=True)
    inv_std = lax.rsqrt(jnp.mean(centre * centre, axis=-1, keepdims=True) + norm_epsilon)
    normed = centre * inv_std
    branch[...] = (normed * gain_v + shift_v).astype(bf16)
    go = grad[...].astype(f32)
    gn = go * gain_v
    gpf = inv_std * (
        gn - jnp.mean(gn, axis=-1, keepdims=True) - normed * jnp.mean(gn * normed, axis=-1, keepdims=True)
    )
    grad[...] = gpf.astype(bf16)
    vec[:, 3 * D : 4 * D] = jnp.sum(gpf, axis=0, keepdims=True)
    vec[:, 4 * D : 5 * D] = jnp.sum(go * normed, axis=0, keepdims=True)
    vec[:, 5 * D : 6 * D] = jnp.sum(go, axis=0, keepdims=True)

    gp_keep[...] = grad[:, pl.ds(pl.multiple_of(p * half, half), half)]
    gp_send[...] = grad[:, pl.ds(pl.multiple_of((1 - p) * half, half), half)]
    write(gp_keep, keep.at[:, pl.ds(0, half)])
    write(gp_send, send.at[:, pl.ds(D, half)])

    def give_back(n, values):
        border[n] = mm(order_t[...], values).astype(bf16)
        first = 0
        for ref, count in ((own, TOK), (row, HALO), (col, HALO), (cor, CORNER)):
            write(border.at[n, pl.ds(first, count), :], ref.at[n])
            first += count

    give_back(0, branch[...])

    @pl.loop(0, 4)
    def _(n):
        cols = pl.ds(pl.multiple_of(n * 256, 256), 256)
        branch[:, cols] = mm_tb(grad[...], wproj[cols, :]).astype(bf16)

    def attend_back(g):
        at = pl.multiple_of(g * LANES, LANES)
        qs = pl.ds(at, LANES)
        v = qkv[:, pl.ds(at + 2 * D, LANES)]
        qu = units[0, :, qs]
        ku = units[1, :, qs]
        gmx = branch[:, qs]
        both = [
            stacked_heads(jnp.concatenate((gmx[rows], qu[rows]), axis=1), mask_pair) for rows in window_rows
        ]
        grad_atts = [mm_tb(v[window_rows[w]], both[w][:, :LANES]) for w in range(WINDOWS)]
        yield
        sc = scale_of(g)
        pos_sum = jnp.zeros((WIN2, WIDE), f32)
        sc_sum = jnp.zeros((WIN2, WIDE), f32)
        pairs, products = [], []
        for w in range(WINDOWS):
            attention = att[g, w]
            att_f = attention.astype(f32)
            dots = jnp.sum(grad_atts[w] * att_f, axis=0, keepdims=True)
            grad_scores = att_f * (grad_atts[w] - dots)
            pos_sum = pos_sum + grad_scores
            sc_sum = sc_sum + grad_scores * cos[g, w]
            grad_cos = (sc * grad_scores).astype(bf16)
            pairs.append(mm(jnp.concatenate((attention, grad_cos), axis=0), both[w]))
            products.append(mm_ta(ku[window_rows[w]], grad_cos))
        yield
        gqu = jnp.concatenate([own_heads(product, f32) for product in products], axis=0)
        gku = jnp.concatenate([pair[WIN2:, LANES:] for pair in pairs], axis=0)
        got = jnp.concatenate((gqu, gku), axis=1)
        inv = jnp.concatenate((inverses[0, :, qs], inverses[1, :, qs]), axis=1)
        unit = jnp.concatenate((qkv[:, qs], qkv[:, pl.ds(at + D, LANES)]), axis=1).astype(f32) * inv
        along = mm((got * unit).astype(bf16), ones)
        yield
        got = inv * (got - unit * along)
        results = [got[:, :LANES], got[:, LANES:], jnp.concatenate([pair[:WIN2, :LANES] for pair in pairs], axis=0)]
        turned = pos_sum.T
        pos_parts = []
        for h in range(GROUP):
            upper = turned[h * WIN2 : h * WIN2 + 32]
            lower = turned[h * WIN2 + 32 : (h + 1) * WIN2]
            pos_parts.append(jnp.concatenate((upper, lower), axis=1))
        pos[pl.ds(pl.multiple_of(g * LANES, LANES), LANES), :] = jnp.concatenate(pos_parts, axis=0)
        vec[:, pl.ds(pl.multiple_of(6 * D + g * WIDE, WIDE), WIDE)] = jnp.sum(sc_sum, axis=0, keepdims=True)
        for n in range(3):
            vec[:, pl.ds(at + n * D, LANES)] = jnp.sum(results[n], axis=0, keepdims=True)
        inner = pl.multiple_of(lax.rem(g, GROUPS // 2) * LANES, LANES)
        yield

        def put(ref):
            for n in range(3):
                ref[:, pl.ds(n * half + inner, LANES)] = results[n].astype(bf16)

        side = g // (GROUPS // 2)
        pl.when(side == p)(lambda: put(g_keep))
        pl.when(side != p)(lambda: put(g_send))

    @pl.loop(0, GROUPS // FUSED)
    def _(n):
        in_step([attend_back(n * FUSED + u) for u in range(FUSED)])

    write(g_keep, keep.at[:, pl.ds(half, 3 * half)])
    write(g_send, send.at[:, pl.ds(5 * half, 3 * half)])

    @pl.loop(0, 64, unroll=8)
    def _(n):
        rows = pl.ds(pl.multiple_of(n * 16, 16), 16)
        tiles = []
        for m in range(2):
            at = pl.multiple_of(lax.rem(2 * n + m, 64) * LANES, LANES)
            tiles.append(jnp.broadcast_to(vec[:, pl.ds(at, LANES)], (8, LANES)))
        small[rows, :] = jnp.concatenate((pos[rows, :], jnp.concatenate(tiles, axis=0)), axis=1).astype(bf16)

    @pl.loop(0, 4)
    def _(n):
        rows = pl.ds(pl.multiple_of(n * 256, 256), 256)
        total = jnp.zeros((TOK, 256), f32)
        for t in range(3):
            for ref, side in ((g_keep, p), (g_send, 1 - p)):
                cols = pl.ds(pl.multiple_of(t * D + side * half, half), half)
                total = total + mm_tb(ref[:, t * half : (t + 1) * half], wqkv[rows, cols])
        branch[:, rows] = total.astype(bf16)

    give_back(1, branch[...])
    for copy in stores:
        copy.wait()


def weight_grad_kernel(mixed, x, mixed_other, x_other, keep, gp_other, q_other, k_other, v_other, out):
    half = D // 2
    a = jnp.concatenate((x[...], x_other[...]), axis=0)
    for t, ref in enumerate((q_other, k_other, v_other)):
        g = jnp.concatenate((keep[:, (t + 1) * half : (t + 2) * half], ref[...]), axis=0)
        out[:, t * half : (t + 1) * half] = mm_ta(a, g).astype(bf16)
    a = jnp.concatenate((mixed[...], mixed_other[...]), axis=0)
    g = jnp.concatenate((keep[:, 0:half], gp_other[...]), axis=0)
    out[:, 3 * half : 4 * half] = mm_ta(a, g).astype(bf16)


def fold_kernel(got, part, part_out, spread_small, sem):
    devices, rows, _ = got.shape
    small = jnp.sum(got[...].astype(f32), axis=0)
    spread_small[...] = jnp.broadcast_to(small[None], (devices, rows, EXTRA)).reshape(D, EXTRA).astype(bf16)
    copy = pltpu.make_async_copy(spread_small, part_out.at[:, pl.ds(2 * D, EXTRA)], sem)
    copy.start()
    copy.wait()


def last_kernel(got, qkv_out, proj_out, pos_out, qkv_bias, proj_bias, gain, shift, scale, total, small):
    half = D // 2
    step = pl.program_id(0)
    pairs, _, rows, _ = got.shape
    count = 2 * pairs * rows

    @pl.when(step == 0)
    def _():
        total[...] = jnp.zeros_like(total)

    for side in range(2):
        total[side] += jnp.sum(got[:, side, :, 0 : 4 * half].astype(f32), axis=0)
    here = got[:, :, :, 4 * half :].astype(f32).reshape(count, EXTRA)
    small[pl.ds(pl.multiple_of(step * count, count), count), :] = here

    @pl.when(step == pl.num_programs(0) - 1)
    def _():
        for side in range(2):
            for t in range(3):
                first = t * D + side * half
                qkv_out[:, first : first + half] = total[side, :, t * half : (t + 1) * half]
            proj_out[:, side * half : (side + 1) * half] = total[side, :, 3 * half :]
        folded = small[:, 0:LANES].reshape(HEADS, WIN2 // 2, LANES)
        pos_out[:, 0 : WIN2 // 2, :] = folded[:, :, 0:WIN2]
        pos_out[:, WIN2 // 2 :, :] = folded[:, :, WIN2:]
        first = 0
        for ref in (qkv_bias, proj_bias, gain, shift):
            for n in range(ref.shape[0] // LANES):
                ref[n * LANES : (n + 1) * LANES] = small[8 * (first + n), LANES:]
            first += ref.shape[0] // LANES
        parts = small[8 * first : 8 * first + LANES, LANES:]
        lane = lax.broadcasted_iota(jnp.int32, (LANES, LANES), 1)
        at = lax.broadcasted_iota(jnp.int32, (LANES, LANES), 0)
        left = jnp.sum(parts[:, :WIN2], axis=1, keepdims=True)
        right = jnp.sum(parts[:, WIN2:], axis=1, keepdims=True)
        heads = jnp.where(at == lane // 2 * 8, jnp.where(lane % 2 == 0, left, right), 0.0)
        heads = jnp.sum(heads, axis=0, keepdims=True)
        scale[...] = heads[0, :HEADS]


def finish_kernel(tok, cot, own, row, col, cor, spread, block_out, grad_tokens):
    for n, (base, out) in enumerate(((tok, block_out), (cot, grad_tokens))):
        border = jnp.concatenate((row[n], col[n], cor[n]), axis=0)
        moved = own[n].astype(f32) + mm(spread[...], border)
        out[...] = (base[...].astype(f32) + moved).astype(bf16)


def sds(shape, dtype):
    return jax.ShapeDtypeStruct(shape, dtype)


VM = pl.BlockSpec(memory_space=pltpu.VMEM)
SM = pl.BlockSpec(memory_space=pltpu.SMEM)
ANY = pl.BlockSpec(memory_space=pl.ANY)


def call(kernel, outs, scratch=(), specs=None, flops=0, bytes_accessed=0, out_specs=None):
    return pl.pallas_call(
        kernel,
        out_shape=outs,
        in_specs=specs,
        out_specs=out_specs or jax.tree.map(lambda _: VM, outs),
        scratch_shapes=list(scratch),
        compiler_params=pltpu.CompilerParams(vmem_limit_bytes=VMEM_LIMIT),
        cost_estimate=pl.CostEstimate(flops=flops, bytes_accessed=bytes_accessed, transcendentals=0),
    )


def neighbour(by_row, by_col):
    rows, cols = lax.axis_size("row"), lax.axis_size("col")
    reps = lax.axis_size("rep")
    pairs = []
    for s in range(reps):
        for r in range(rows):
            for c in range(cols):
                to = (s * rows + (r + by_row) % rows) * cols + (c + by_col) % cols
                pairs.append(((s * rows + r) * cols + c, to))
    return pairs


def per_device(
    tokens, cotangent, row_field, col_field, qkv_weight, qkv_bias, logit_scale, position_bias,
    proj_weight, proj_bias, norm_gain, norm_shift,
):
    devices = lax.axis_size(AXES)
    order = jnp.asarray(window_order(), bf16)
    order_t = jnp.asarray(window_order().T, bf16)
    spread = jnp.asarray(border_spread(), bf16)
    spread_t = jnp.asarray(border_spread().T, bf16)
    mask = jnp.asarray(head_mask(), bf16)
    ones = jnp.asarray(head_sums(), bf16)
    tok = tokens[0].reshape(TOK, D)
    cot = cotangent[0].reshape(TOK, D)

    row_in, col_in, cor_in = call(
        pack_kernel, (sds((2, HALO, D), bf16), sds((2, HALO, D), bf16), sds((2, CORNER, D), bf16)), (), [VM] * 3,
        flops=10**8, bytes_accessed=2**21,
    )(tok, cot, spread_t)
    row_in = lax.ppermute(row_in, AXES, neighbour(-1, 0))
    col_in = lax.ppermute(col_in, AXES, neighbour(0, -1))
    cor_in = lax.ppermute(cor_in, AXES, neighbour(-1, -1))

    col_index = lax.axis_index("col")
    place = jnp.stack((lax.axis_index("row") * SIDE, col_index * SIDE, col_index % 2)).astype(jnp.int32)
    bias_t = position_bias.reshape(GROUPS, GROUP, WIN2, WIN2).transpose(0, 3, 1, 2).reshape(GROUPS, WIN2, WIDE)

    send, keep, own, row, col, cor, small = call(
        local_kernel,
        (
            sds((TOK, 4 * D), bf16), sds((TOK, 2 * D), bf16),
            sds((2, TOK, D), bf16), sds((2, HALO, D), bf16), sds((2, HALO, D), bf16), sds((2, CORNER, D), bf16),
            sds((D, EXTRA), bf16),
        ),
        [
            pltpu.VMEM((D, 3 * D), bf16), pltpu.VMEM((D, D), bf16), pltpu.VMEM((GROUPS, WIN2, WIDE), f32),
            pltpu.VMEM((CAT, D), bf16), pltpu.VMEM((TOK, 3 * D), bf16),
            pltpu.VMEM((GROUPS, WINDOWS, WIN2, WIDE), bf16), pltpu.VMEM((GROUPS, WINDOWS, WIN2, WIDE), f32),
            pltpu.VMEM((2, TOK, D), bf16), pltpu.VMEM((2, TOK, D), f32), pltpu.VMEM((TOK, D), bf16),
            pltpu.VMEM((TOK, D), f32), pltpu.VMEM((TOK, D), bf16), pltpu.VMEM((HEADS * 32, LANES), f32),
            pltpu.VMEM((1, 8 * D), f32), pltpu.VMEM((TOK, D), bf16), pltpu.VMEM((TOK, D), bf16),
            pltpu.VMEM((TOK, D // 2), bf16), pltpu.VMEM((TOK, D // 2), bf16), pltpu.VMEM((TOK, 3 * D // 2), bf16),
            pltpu.VMEM((TOK, 3 * D // 2), bf16), pltpu.VMEM((2, CAT, D), bf16),
            pltpu.SemaphoreType.DMA((5,)), pltpu.SemaphoreType.DMA((14,)),
        ],
        [SM] * 4 + [VM] * 9 + [ANY, VM, ANY, ANY, VM, VM, VM],
        flops=5 * 10**9, bytes_accessed=20 * 2**20, out_specs=(ANY,) * 6 + (VM,),
    )(
        place, row_field, col_field, logit_scale, tok, cot, row_in, col_in, cor_in, order, order_t, mask, ones,
        qkv_weight, qkv_bias.reshape(1, -1), bias_t, proj_weight, proj_bias.reshape(1, -1),
        norm_gain.reshape(1, -1), norm_shift.reshape(1, -1),
    )
    cores = [(i, i ^ 1) for i in range(lax.axis_size("col"))]
    other = lax.ppermute(send, "col", cores)
    rows = D // devices
    small = lax.all_to_all(small.reshape(devices, rows, EXTRA), AXES, 0, 0, tiled=True)
    row = lax.ppermute(row, AXES, neighbour(1, 0))
    col = lax.ppermute(col, AXES, neighbour(0, 1))
    cor = lax.ppermute(cor, AXES, neighbour(1, 1))
    block = D // 2

    def columns(first, moving):
        return pl.BlockSpec((TOK, block), lambda i: (0, first + (i if moving else 0)))

    part = pl.pallas_call(
        weight_grad_kernel,
        grid=(2,),
        out_shape=sds((D, 2 * D + EXTRA), bf16),
        in_specs=[
            columns(0, True), columns(3, True), columns(0, True), columns(3, True),
            pl.BlockSpec((TOK, 2 * D), lambda i: (0, 0)),
            columns(2, False), columns(5, False), columns(6, False), columns(7, False),
        ],
        out_specs=pl.BlockSpec((block, 2 * D + EXTRA), lambda i: (i, 0)),
        compiler_params=pltpu.CompilerParams(vmem_limit_bytes=VMEM_LIMIT),
        cost_estimate=pl.CostEstimate(flops=8 * TOK * D * D, bytes_accessed=8 * 2**20, transcendentals=0),
    )(send, send, other, other, keep, other, other, other, other)
    part, small = lax.optimization_barrier((part, small))
    part = pl.pallas_call(
        fold_kernel,
        out_shape=sds(part.shape, bf16),
        in_specs=[VM, ANY],
        out_specs=ANY,
        scratch_shapes=[pltpu.VMEM((D, EXTRA), bf16), pltpu.SemaphoreType.DMA],
        input_output_aliases={1: 0},
        compiler_params=pltpu.CompilerParams(vmem_limit_bytes=VMEM_LIMIT),
        cost_estimate=pl.CostEstimate(flops=10**6, bytes_accessed=2**20, transcendentals=0),
    )(small, part)
    part, row, col, cor = lax.optimization_barrier((part, row, col, cor))
    got = lax.all_to_all(part.reshape(devices, rows, -1), AXES, 0, 0, tiled=True)
    block_out, grad_tokens = call(
        finish_kernel, (sds((TOK, D), bf16), sds((TOK, D), bf16)), (), [VM] * 7, flops=10**8, bytes_accessed=2**22
    )(tok, cot, own, row, col, cor, spread)
    steps = 1
    outs = (
        sds((rows, 3 * D), f32), sds((rows, D), f32), sds((HEADS, WIN2, WIN2), f32), sds((3 * D,), f32), sds((D,), f32),
        sds((D,), f32), sds((D,), f32), sds((HEADS,), f32),
    )
    grad_qkv_weight, grad_proj_weight, grad_position, g_qkv_bias, g_proj_bias, g_gain, g_shift, g_scale = pl.pallas_call(
        last_kernel,
        grid=(steps,),
        out_shape=outs,
        in_specs=[pl.BlockSpec((devices // 2 // steps, 2, rows, got.shape[2]), lambda i: (i, 0, 0, 0))],
        out_specs=tuple(pl.BlockSpec(o.shape, lambda i, n=len(o.shape): (0,) * n) for o in outs),
        scratch_shapes=[pltpu.VMEM((2, rows, 2 * D), f32), pltpu.VMEM((D, EXTRA), f32)],
        compiler_params=pltpu.CompilerParams(vmem_limit_bytes=VMEM_LIMIT),
        cost_estimate=pl.CostEstimate(flops=10**7, bytes_accessed=2**22, transcendentals=0),
    )(got.reshape(devices // 2, 2, rows, -1))
    return (
        block_out.reshape(1, SIDE, SIDE, D), grad_tokens.reshape(1, SIDE, SIDE, D), grad_qkv_weight, grad_proj_weight, g_qkv_bias, g_proj_bias,
        g_gain, g_shift, g_scale, grad_position,
    )


def solution(mesh):
    grid = P("rep", "row", "col", None)
    rows = P(AXES, None)
    return jax.shard_map(
        per_device,
        mesh=mesh,
        in_specs=(grid, grid, P("rep", None), P("rep", None)) + (P(),) * 8,
        out_specs=(grid, grid, rows, rows) + (P(),) * 6,
        check_vma=False,
    )
```

```python
import functools

import jax
import jax.numpy as jnp
import numpy as np
from jax import lax
from jax.experimental import pallas as pl
from jax.experimental.pallas import tpu as pltpu
from jax.sharding import PartitionSpec as P

HEADS = 32
WIN = 8
SHIFT = 4
SIDE = 16
TOK = SIDE * SIDE
D = 1024
HALO = (SIDE - SHIFT) * SHIFT
CORNER = SHIFT * SHIFT
BORDER = 2 * HALO + CORNER
CAT = TOK + BORDER
WIN2 = WIN * WIN
WINDOWS = TOK // WIN2
GROUP = 4
GROUPS = HEADS // GROUP
LANES = 128
WIDE = GROUP * WIN2
FUSED = 8
EXTRA = 2 * LANES
AXES = ("rep", "row", "col")

norm_epsilon = 1e-05
unit_floor = 1e-12
f32 = jnp.float32
bf16 = jnp.bfloat16
VMEM_LIMIT = 56 * 1024 * 1024


def window_order():
    order = np.zeros((TOK, CAT), np.float32)
    for r in range(SIDE):
        for c in range(SIDE):
            n = ((r // WIN) * 2 + c // WIN) * WIN2 + (r % WIN) * WIN + c % WIN
            rr, cc = r + SHIFT, c + SHIFT
            if rr < SIDE and cc < SIDE:
                m = rr * SIDE + cc
            elif cc < SIDE:
                m = TOK + (rr - SIDE) * (SIDE - SHIFT) + cc - SHIFT
            elif rr < SIDE:
                m = TOK + HALO + (rr - SHIFT) * SHIFT + (cc - SIDE)
            else:
                m = TOK + 2 * HALO + (rr - SIDE) * SHIFT + (cc - SIDE)
            order[n, m] = 1.0
    return order


def border_spread():
    spread = np.zeros((TOK, BORDER), np.float32)
    for r in range(SIDE):
        for c in range(SIDE):
            if r < SHIFT and c >= SHIFT:
                spread[r * SIDE + c, r * (SIDE - SHIFT) + c - SHIFT] = 1.0
            elif r >= SHIFT and c < SHIFT:
                spread[r * SIDE + c, HALO + (r - SHIFT) * SHIFT + c] = 1.0
            elif r < SHIFT and c < SHIFT:
                spread[r * SIDE + c, 2 * HALO + r * SHIFT + c] = 1.0
    return spread


def head_mask():
    rows = np.arange(WIDE)[:, None] // WIN2
    cols = np.arange(LANES)[None, :] // (LANES // GROUP)
    return (rows == cols).astype(np.float32)


def head_sums():
    heads = np.arange(2 * LANES) // (LANES // GROUP)
    return (heads[:, None] == heads[None, :]).astype(np.float32)


def mm(a, b):
    return jnp.dot(a, b, preferred_element_type=f32)


def mm_tb(a, b):
    return lax.dot_general(a, b, (((1,), (1,)), ((), ())), preferred_element_type=f32)


def mm_ta(a, b):
    return lax.dot_general(a, b, (((0,), (0,)), ((), ())), preferred_element_type=f32)


def exact_sums(values, ones):
    high = values.astype(bf16)
    low = (values - high.astype(f32)).astype(bf16)
    return mm(high, ones) + mm(low, ones)


def stacked_heads(x, mask):
    return jnp.concatenate((x, x, x, x), axis=0) * mask


def in_step(parts):
    while parts:
        parts = [part for part in parts if next(part, parts) is not parts]


def split_border(border, n, row, col, cor):
    row[n] = border[:HALO]
    col[n] = border[HALO : 2 * HALO]
    cor[n] = border[2 * HALO :]


def pack_kernel(tok, cot, spread_t, row, col, cor):
    for n, ref in enumerate((tok, cot)):
        split_border(mm(spread_t[...], ref[...]).astype(bf16), n, row, col, cor)


def local_kernel(
    place, row_field, col_field, logit_scale, tok, cot, row_in, col_in, cor_in, order, order_t, mask_ref, ones_ref,
    wqkv_hbm, bqkv, bias_hbm, wproj_hbm, bproj, gain, shift,
    send, keep, own, row, col, cor, small,
    wqkv, wproj, bias_t, cat, qkv, att, cos, units, inverses, grad, wide, branch, pos, vec,
    x, mixed, gp_send, gp_keep, g_send, g_keep, border, sems, out_sems,
):
    loads = []

    def load(source, target):
        copy = pltpu.make_async_copy(source, target, sems.at[len(loads)])
        copy.start()
        loads.append(copy)
        return copy

    def gather(n, whole):
        first, copies = 0, []
        for source, count in ((whole, TOK), (row_in.at[n], HALO), (col_in.at[n], HALO), (cor_in.at[n], CORNER)):
            copies.append(load(source, cat.at[n, pl.ds(first, count), :]))
            first += count
        return copies

    tok_loads = gather(0, tok)
    weight_loads = [load(wqkv_hbm.at[:, pl.ds(t * D, D)], wqkv.at[:, pl.ds(t * D, D)]) for t in range(3)]
    bias_load = load(bias_hbm, bias_t)
    cot_loads = gather(1, cot)
    proj_load = load(wproj_hbm, wproj)

    p = place[2]
    half = D // 2
    stores = []

    def write(source, target):
        copy = pltpu.make_async_copy(source, target, out_sems.at[len(stores)])
        copy.start()
        stores.append(copy)

    for copy in tok_loads:
        copy.wait()
    x[...] = mm(order[...], cat[0]).astype(bf16)
    write(x, send.at[:, pl.ds(3 * half, D)])

    sub = lax.broadcasted_iota(jnp.int32, (WIN2, WIDE), 0)
    lane = lax.broadcasted_iota(jnp.int32, (WIN2, WIDE), 1) % WIN2
    row_ids, col_ids = [], []
    for i in range(SIDE):
        row_ids.append(row_field[0, lax.rem(place[0] + SHIFT + i, row_field.shape[1])] * 1024)
        col_ids.append(col_field[0, lax.rem(place[1] + SHIFT + i, col_field.shape[1])])

    def spread_ids(ids, index):
        out = jnp.zeros((WIN2, WIDE), jnp.int32)
        for i in range(WIN):
            out = jnp.where(index == i, ids[i], out)
        return out

    row_same, col_same = [], []
    for n in range(2):
        part = slice(n * WIN, (n + 1) * WIN)
        row_same.append(spread_ids(row_ids[part], sub // WIN) == spread_ids(row_ids[part], lane // WIN))
        col_same.append(spread_ids(col_ids[part], sub % WIN) == spread_ids(col_ids[part], lane % WIN))
    allowed = [(row_same[w // 2] & col_same[w % 2]).astype(f32) for w in range(WINDOWS)]
    mask = mask_ref[...]
    mask_pair = jnp.concatenate((mask, mask), axis=1)
    ones = ones_ref[...]
    wide_lane = lax.broadcasted_iota(jnp.int32, (1, WIDE), 1) // WIN2

    odd_head = lax.broadcasted_iota(jnp.int32, (WIN2, LANES), 1) // (LANES // GROUP) % 2 == 1

    def own_heads(full, dtype):
        picked = jnp.concatenate((full[:WIN2, :LANES], full[WIN2:, LANES:]), axis=0).astype(dtype).T
        return jnp.where(odd_head, picked[WIN2:], picked[:WIN2])

    head_lane = lax.broadcasted_iota(jnp.int32, (WIN2, LANES), 1) // (LANES // GROUP)

    def pick_heads(full):
        out = full[:WIN2]
        for h in range(1, GROUP):
            out = jnp.where(head_lane == h, full[h * WIN2 : (h + 1) * WIN2], out)
        return out

    window_rows = [slice(w * WIN2, (w + 1) * WIN2) for w in range(WINDOWS)]

    def scale_of(g):
        out = jnp.zeros((1, WIDE), f32)
        for h in range(GROUP):
            out = jnp.where(wide_lane == h, logit_scale[g * GROUP + h], out)
        return out

    for t in range(3):
        weight_loads[t].wait()

        @pl.loop(0, 2)
        def _(n):
            cols = pl.ds(pl.multiple_of(t * D + n * 512, 512), 512)
            qkv[:, cols] = (mm(x[...], wqkv[:, cols]) + bqkv[:, cols]).astype(bf16)

    bias_load.wait()

    def attend(g):
        at = pl.multiple_of(g * LANES, LANES)
        qs = pl.ds(at, LANES)
        v = qkv[:, pl.ds(at + 2 * D, LANES)]
        raw = jnp.concatenate((qkv[:, qs], qkv[:, pl.ds(at + D, LANES)]), axis=1).astype(f32)
        total = exact_sums(raw * raw, ones)
        yield
        inv = lax.rsqrt(jnp.maximum(total, unit_floor * unit_floor))
        unit = (raw * inv).astype(bf16)
        qu, ku = unit[:, :LANES], unit[:, LANES:]
        cosines = [mm_tb(ku[rows], stacked_heads(qu[rows], mask)) for rows in window_rows]
        yield
        sc = scale_of(g)
        bias = bias_t[g]
        attentions = []
        for w in range(WINDOWS):
            weights = jnp.exp(sc * cosines[w] + bias) * allowed[w]
            total = jnp.sum(weights, axis=0, keepdims=True)
            attentions.append((weights * (1.0 / total)).astype(bf16))
        products = [mm_ta(attentions[w], v[window_rows[w]]) for w in range(WINDOWS)]
        yield
        for n in range(2):
            inverses[n, :, qs] = inv[:, n * LANES : (n + 1) * LANES]
            units[n, :, qs] = unit[:, n * LANES : (n + 1) * LANES]
        for w in range(WINDOWS):
            att[g, w] = attentions[w]
            cos[g, w] = cosines[w]
        mixed[:, qs] = jnp.concatenate([pick_heads(product).astype(bf16) for product in products], axis=0)

    @pl.loop(0, GROUPS // FUSED)
    def _(n):
        in_step([attend(n * FUSED + u) for u in range(FUSED)])

    write(mixed, send.at[:, pl.ds(0, D)])
    proj_load.wait()
    for copy in cot_loads:
        copy.wait()
    grad[...] = mm(order[...], cat[1]).astype(bf16)

    @pl.loop(0, 4)
    def _(n):
        cols = pl.ds(pl.multiple_of(n * 256, 256), 256)
        wide[:, cols] = mm(mixed[...], wproj[:, cols]) + bproj[:, cols]

    gain_v = gain[...]
    shift_v = shift[...]

    projected = wide[...]
    centre = projected - jnp.mean(projected, axis=-1, keepdims=True)
    inv_std = lax.rsqrt(jnp.mean(centre * centre, axis=-1, keepdims=True) + norm_epsilon)
    normed = centre * inv_std
    branch[...] = (normed * gain_v + shift_v).astype(bf16)
    go = grad[...].astype(f32)
    gn = go * gain_v
    gpf = inv_std * (
        gn - jnp.mean(gn, axis=-1, keepdims=True) - normed * jnp.mean(gn * normed, axis=-1, keepdims=True)
    )
    grad[...] = gpf.astype(bf16)
    vec[:, 3 * D : 4 * D] = jnp.sum(gpf, axis=0, keepdims=True)
    vec[:, 4 * D : 5 * D] = jnp.sum(go * normed, axis=0, keepdims=True)
    vec[:, 5 * D : 6 * D] = jnp.sum(go, axis=0, keepdims=True)

    gp_keep[...] = grad[:, pl.ds(pl.multiple_of(p * half, half), half)]
    gp_send[...] = grad[:, pl.ds(pl.multiple_of((1 - p) * half, half), half)]
    write(gp_keep, keep.at[:, pl.ds(0, half)])
    write(gp_send, send.at[:, pl.ds(D, half)])

    def give_back(n, values):
        border[n] = mm(order_t[...], values).astype(bf16)
        first = 0
        for ref, count in ((own, TOK), (row, HALO), (col, HALO), (cor, CORNER)):
            write(border.at[n, pl.ds(first, count), :], ref.at[n])
            first += count

    give_back(0, branch[...])

    @pl.loop(0, 4)
    def _(n):
        cols = pl.ds(pl.multiple_of(n * 256, 256), 256)
        branch[:, cols] = mm_tb(grad[...], wproj[cols, :]).astype(bf16)

    def attend_back(g):
        at = pl.multiple_of(g * LANES, LANES)
        qs = pl.ds(at, LANES)
        v = qkv[:, pl.ds(at + 2 * D, LANES)]
        qu = units[0, :, qs]
        ku = units[1, :, qs]
        gmx = branch[:, qs]
        both = [
            stacked_heads(jnp.concatenate((gmx[rows], qu[rows]), axis=1), mask_pair) for rows in window_rows
        ]
        grad_atts = [mm_tb(v[window_rows[w]], both[w][:, :LANES]) for w in range(WINDOWS)]
        yield
        sc = scale_of(g)
        pos_sum = jnp.zeros((WIN2, WIDE), f32)
        sc_sum = jnp.zeros((WIN2, WIDE), f32)
        pairs, products = [], []
        for w in range(WINDOWS):
            attention = att[g, w]
            att_f = attention.astype(f32)
            dots = jnp.sum(grad_atts[w] * att_f, axis=0, keepdims=True)
            grad_scores = att_f * (grad_atts[w] - dots)
            pos_sum = pos_sum + grad_scores
            sc_sum = sc_sum + grad_scores * cos[g, w]
            grad_cos = (sc * grad_scores).astype(bf16)
            pairs.append(mm(jnp.concatenate((attention, grad_cos), axis=0), both[w]))
            products.append(mm_ta(ku[window_rows[w]], grad_cos))
        yield
        gqu = jnp.concatenate([own_heads(product, f32) for product in products], axis=0)
        gku = jnp.concatenate([pair[WIN2:, LANES:] for pair in pairs], axis=0)
        got = jnp.concatenate((gqu, gku), axis=1)
        inv = jnp.concatenate((inverses[0, :, qs], inverses[1, :, qs]), axis=1)
        unit = jnp.concatenate((qkv[:, qs], qkv[:, pl.ds(at + D, LANES)]), axis=1).astype(f32) * inv
        along = mm((got * unit).astype(bf16), ones)
        yield
        got = inv * (got - unit * along)
        results = [got[:, :LANES], got[:, LANES:], jnp.concatenate([pair[:WIN2, :LANES] for pair in pairs], axis=0)]
        turned = pos_sum.T
        pos_parts = []
        for h in range(GROUP):
            upper = turned[h * WIN2 : h * WIN2 + 32]
            lower = turned[h * WIN2 + 32 : (h + 1) * WIN2]
            pos_parts.append(jnp.concatenate((upper, lower), axis=1))
        pos[pl.ds(pl.multiple_of(g * LANES, LANES), LANES), :] = jnp.concatenate(pos_parts, axis=0)
        vec[:, pl.ds(pl.multiple_of(6 * D + g * WIDE, WIDE), WIDE)] = jnp.sum(sc_sum, axis=0, keepdims=True)
        for n in range(3):
            vec[:, pl.ds(at + n * D, LANES)] = jnp.sum(results[n], axis=0, keepdims=True)
        inner = pl.multiple_of(lax.rem(g, GROUPS // 2) * LANES, LANES)
        yield

        def put(ref):
            for n in range(3):
                ref[:, pl.ds(n * half + inner, LANES)] = results[n].astype(bf16)

        side = g // (GROUPS // 2)
        pl.when(side == p)(lambda: put(g_keep))
        pl.when(side != p)(lambda: put(g_send))

    @pl.loop(0, GROUPS // FUSED)
    def _(n):
        in_step([attend_back(n * FUSED + u) for u in range(FUSED)])

    write(g_keep, keep.at[:, pl.ds(half, 3 * half)])
    write(g_send, send.at[:, pl.ds(5 * half, 3 * half)])

    @pl.loop(0, 64, unroll=8)
    def _(n):
        rows = pl.ds(pl.multiple_of(n * 16, 16), 16)
        tiles = []
        for m in range(2):
            at = pl.multiple_of(lax.rem(2 * n + m, 64) * LANES, LANES)
            tiles.append(jnp.broadcast_to(vec[:, pl.ds(at, LANES)], (8, LANES)))
        small[rows, :] = jnp.concatenate((pos[rows, :], jnp.concatenate(tiles, axis=0)), axis=1).astype(bf16)

    @pl.loop(0, 4)
    def _(n):
        rows = pl.ds(pl.multiple_of(n * 256, 256), 256)
        total = jnp.zeros((TOK, 256), f32)
        for t in range(3):
            for ref, side in ((g_keep, p), (g_send, 1 - p)):
                cols = pl.ds(pl.multiple_of(t * D + side * half, half), half)
                total = total + mm_tb(ref[:, t * half : (t + 1) * half], wqkv[rows, cols])
        branch[:, rows] = total.astype(bf16)

    give_back(1, branch[...])
    for copy in stores:
        copy.wait()


def weight_grad_kernel(send, keep, other, out, own_v, other_v, keep_v, part, in_sems, out_sems):
    half = D // 2
    loads, stores = [], []

    def load(source, target, first, width):
        cols = pl.ds(first, width)
        copy = pltpu.make_async_copy(source.at[:, cols], target.at[:, cols], in_sems.at[len(loads)])
        copy.start()
        loads.append(copy)

    load(send, own_v, 3 * half, D)
    load(keep, keep_v, half, half)
    load(other, other_v, 3 * half, D)
    load(other, other_v, 5 * half, half)
    load(keep, keep_v, D, D)
    load(other, other_v, 6 * half, D)
    load(send, own_v, 0, D)
    load(other, other_v, 0, 3 * half)
    load(keep, keep_v, 0, half)

    def multiply(t, feature, grad_keep, grad_other):
        grad = jnp.concatenate(
            (keep_v[:, grad_keep : grad_keep + half], other_v[:, grad_other : grad_other + half]), axis=0
        )
        for m in range(2):
            cols = slice(feature + m * half, feature + (m + 1) * half)
            value = jnp.concatenate((own_v[:, cols], other_v[:, cols]), axis=0)
            part[t, m * half : (m + 1) * half, :] = mm_ta(value, grad).astype(bf16)
        copy = pltpu.make_async_copy(part.at[t], out.at[:, pl.ds(t * half, half)], out_sems.at[t])
        copy.start()
        stores.append(copy)

    for n in range(4):
        loads[n].wait()
    multiply(0, 3 * half, half, 5 * half)
    for n in range(4, 6):
        loads[n].wait()
    multiply(1, 3 * half, 2 * half, 6 * half)
    multiply(2, 3 * half, 3 * half, 7 * half)
    for n in range(6, 9):
        loads[n].wait()
    multiply(3, 0, 0, 2 * half)
    for copy in stores:
        copy.wait()


def last_kernel(
    got_hbm, qkv_out, proj_out, pos_out, qkv_bias, proj_bias, gain, shift, scale, got, total, small, sems
):
    half = D // 2
    pairs, _, rows, _ = got.shape
    steps = sems.shape[0]
    each = pairs // steps
    loads = []
    for n in range(steps):
        part = pl.ds(n * each, each)
        loads.append(pltpu.make_async_copy(got_hbm.at[part], got.at[part], sems.at[n]))
        loads[n].start()
    for n in range(steps):
        loads[n].wait()
        here = slice(n * each, (n + 1) * each)
        for side in range(2):
            value = jnp.sum(got[here, side, :, 0 : 4 * half].astype(f32), axis=0)
            total[side] = value if n == 0 else total[side] + value
        count = 2 * each * rows
        small[n * count : (n + 1) * count, :] = got[here, :, :, 4 * half :].astype(f32).reshape(count, EXTRA)
    for side in range(2):
        for t in range(3):
            first = t * D + side * half
            qkv_out[:, first : first + half] = total[side, :, t * half : (t + 1) * half]
        proj_out[:, side * half : (side + 1) * half] = total[side, :, 3 * half :]
    folded = small[:, 0:LANES].reshape(HEADS, WIN2 // 2, LANES)
    pos_out[:, 0 : WIN2 // 2, :] = folded[:, :, 0:WIN2]
    pos_out[:, WIN2 // 2 :, :] = folded[:, :, WIN2:]
    first = 0
    for ref in (qkv_bias, proj_bias, gain, shift):
        for n in range(ref.shape[0] // LANES):
            ref[n * LANES : (n + 1) * LANES] = small[8 * (first + n), LANES:]
        first += ref.shape[0] // LANES
    parts = small[8 * first : 8 * first + LANES, LANES:]
    lane = lax.broadcasted_iota(jnp.int32, (LANES, LANES), 1)
    at = lax.broadcasted_iota(jnp.int32, (LANES, LANES), 0)
    left = jnp.sum(parts[:, :WIN2], axis=1, keepdims=True)
    right = jnp.sum(parts[:, WIN2:], axis=1, keepdims=True)
    heads = jnp.where(at == lane // 2 * 8, jnp.where(lane % 2 == 0, left, right), 0.0)
    heads = jnp.sum(heads, axis=0, keepdims=True)
    scale[...] = heads[0, :HEADS]


def finish_kernel(tok, cot, own, row, col, cor, spread, block_out, grad_tokens):
    for n, (base, out) in enumerate(((tok, block_out), (cot, grad_tokens))):
        border = jnp.concatenate((row[n], col[n], cor[n]), axis=0)
        moved = own[n].astype(f32) + mm(spread[...], border)
        out[...] = (base[...].astype(f32) + moved).astype(bf16)


def sds(shape, dtype):
    return jax.ShapeDtypeStruct(shape, dtype)


VM = pl.BlockSpec(memory_space=pltpu.VMEM)
SM = pl.BlockSpec(memory_space=pltpu.SMEM)
ANY = pl.BlockSpec(memory_space=pl.ANY)


def call(kernel, outs, scratch=(), specs=None, flops=0, bytes_accessed=0, out_specs=None):
    return pl.pallas_call(
        kernel,
        out_shape=outs,
        in_specs=specs,
        out_specs=out_specs or jax.tree.map(lambda _: VM, outs),
        scratch_shapes=list(scratch),
        compiler_params=pltpu.CompilerParams(vmem_limit_bytes=VMEM_LIMIT),
        cost_estimate=pl.CostEstimate(flops=flops, bytes_accessed=bytes_accessed, transcendentals=0),
    )


def neighbour(by_row, by_col):
    rows, cols = lax.axis_size("row"), lax.axis_size("col")
    reps = lax.axis_size("rep")
    pairs = []
    for s in range(reps):
        for r in range(rows):
            for c in range(cols):
                to = (s * rows + (r + by_row) % rows) * cols + (c + by_col) % cols
                pairs.append(((s * rows + r) * cols + c, to))
    return pairs


def per_device(
    tokens, cotangent, row_field, col_field, qkv_weight, qkv_bias, logit_scale, position_bias,
    proj_weight, proj_bias, norm_gain, norm_shift,
):
    devices = lax.axis_size(AXES)
    order = jnp.asarray(window_order(), bf16)
    order_t = jnp.asarray(window_order().T, bf16)
    spread = jnp.asarray(border_spread(), bf16)
    spread_t = jnp.asarray(border_spread().T, bf16)
    mask = jnp.asarray(head_mask(), bf16)
    ones = jnp.asarray(head_sums(), bf16)
    tok = tokens[0].reshape(TOK, D)
    cot = cotangent[0].reshape(TOK, D)

    row_in, col_in, cor_in = call(
        pack_kernel, (sds((2, HALO, D), bf16), sds((2, HALO, D), bf16), sds((2, CORNER, D), bf16)), (), [VM] * 3,
        flops=10**8, bytes_accessed=2**21,
    )(tok, cot, spread_t)
    row_in = lax.ppermute(row_in, AXES, neighbour(-1, 0))
    col_in = lax.ppermute(col_in, AXES, neighbour(0, -1))
    cor_in = lax.ppermute(cor_in, AXES, neighbour(-1, -1))

    col_index = lax.axis_index("col")
    place = jnp.stack((lax.axis_index("row") * SIDE, col_index * SIDE, col_index % 2)).astype(jnp.int32)
    bias_t = position_bias.reshape(GROUPS, GROUP, WIN2, WIN2).transpose(0, 3, 1, 2).reshape(GROUPS, WIN2, WIDE)

    send, keep, own, row, col, cor, small = call(
        local_kernel,
        (
            sds((TOK, 4 * D), bf16), sds((TOK, 2 * D), bf16),
            sds((2, TOK, D), bf16), sds((2, HALO, D), bf16), sds((2, HALO, D), bf16), sds((2, CORNER, D), bf16),
            sds((D, EXTRA), bf16),
        ),
        [
            pltpu.VMEM((D, 3 * D), bf16), pltpu.VMEM((D, D), bf16), pltpu.VMEM((GROUPS, WIN2, WIDE), f32),
            pltpu.VMEM((2, CAT, D), bf16), pltpu.VMEM((TOK, 3 * D), bf16),
            pltpu.VMEM((GROUPS, WINDOWS, WIN2, WIDE), bf16), pltpu.VMEM((GROUPS, WINDOWS, WIN2, WIDE), f32),
            pltpu.VMEM((2, TOK, D), bf16), pltpu.VMEM((2, TOK, D), f32), pltpu.VMEM((TOK, D), bf16),
            pltpu.VMEM((TOK, D), f32), pltpu.VMEM((TOK, D), bf16), pltpu.VMEM((HEADS * 32, LANES), f32),
            pltpu.VMEM((1, 8 * D), f32), pltpu.VMEM((TOK, D), bf16), pltpu.VMEM((TOK, D), bf16),
            pltpu.VMEM((TOK, D // 2), bf16), pltpu.VMEM((TOK, D // 2), bf16), pltpu.VMEM((TOK, 3 * D // 2), bf16),
            pltpu.VMEM((TOK, 3 * D // 2), bf16), pltpu.VMEM((2, CAT, D), bf16),
            pltpu.SemaphoreType.DMA((13,)), pltpu.SemaphoreType.DMA((14,)),
        ],
        [SM] * 4 + [ANY] * 5 + [VM] * 4 + [ANY, VM, ANY, ANY, VM, VM, VM],
        flops=5 * 10**9, bytes_accessed=20 * 2**20, out_specs=(ANY,) * 6 + (VM,),
    )(
        place, row_field, col_field, logit_scale, tok, cot, row_in, col_in, cor_in, order, order_t, mask, ones,
        qkv_weight, qkv_bias.reshape(1, -1), bias_t, proj_weight, proj_bias.reshape(1, -1),
        norm_gain.reshape(1, -1), norm_shift.reshape(1, -1),
    )
    cores = [(i, i ^ 1) for i in range(lax.axis_size("col"))]
    other = lax.ppermute(send, "col", cores)
    rows = D // devices
    small = lax.all_to_all(small.reshape(devices, rows, EXTRA), AXES, 0, 0, tiled=True)
    row = lax.ppermute(row, AXES, neighbour(1, 0))
    col = lax.ppermute(col, AXES, neighbour(0, 1))
    cor = lax.ppermute(cor, AXES, neighbour(1, 1))
    part = call(
        weight_grad_kernel,
        sds((D, 2 * D + EXTRA), bf16),
        [
            pltpu.VMEM((TOK, 4 * D), bf16), pltpu.VMEM((TOK, 4 * D), bf16), pltpu.VMEM((TOK, 2 * D), bf16),
            pltpu.VMEM((4, D, D // 2), bf16), pltpu.SemaphoreType.DMA((9,)), pltpu.SemaphoreType.DMA((4,)),
        ],
        [ANY] * 3,
        flops=8 * TOK * D * D, bytes_accessed=9 * 2**20, out_specs=ANY,
    )(send, keep, other)
    part, small = lax.optimization_barrier((part.reshape(devices, rows, -1), small))
    small = jnp.sum(small.astype(f32), axis=0).astype(bf16)
    part = part.at[:, :, 2 * D :].set(jnp.broadcast_to(small[None], (devices, rows, EXTRA)))
    part, row, col, cor = lax.optimization_barrier((part, row, col, cor))
    got = lax.all_to_all(part, AXES, 0, 0, tiled=True)
    block_out, grad_tokens = call(
        finish_kernel, (sds((TOK, D), bf16), sds((TOK, D), bf16)), (), [VM] * 7, flops=10**8, bytes_accessed=2**22
    )(tok, cot, own, row, col, cor, spread)
    outs = (
        sds((rows, 3 * D), f32), sds((rows, D), f32), sds((HEADS, WIN2, WIN2), f32), sds((3 * D,), f32), sds((D,), f32),
        sds((D,), f32), sds((D,), f32), sds((HEADS,), f32),
    )
    got = got.reshape(devices // 2, 2, rows, 2 * D + EXTRA)
    steps = min(4, devices // 2)
    grad_qkv_weight, grad_proj_weight, grad_position, g_qkv_bias, g_proj_bias, g_gain, g_shift, g_scale = call(
        last_kernel,
        outs,
        [
            pltpu.VMEM(got.shape, bf16), pltpu.VMEM((2, rows, 2 * D), f32), pltpu.VMEM((D, EXTRA), f32),
            pltpu.SemaphoreType.DMA((steps,)),
        ],
        [ANY],
        flops=10**7, bytes_accessed=2**22,
    )(got)
    return (
        block_out.reshape(1, SIDE, SIDE, D), grad_tokens.reshape(1, SIDE, SIDE, D), grad_qkv_weight, grad_proj_weight, g_qkv_bias, g_proj_bias,
        g_gain, g_shift, g_scale, grad_position,
    )


def solution(mesh):
    grid = P("rep", "row", "col", None)
    rows = P(AXES, None)
    return jax.shard_map(
        per_device,
        mesh=mesh,
        in_specs=(grid, grid, P("rep", None), P("rep", None)) + (P(),) * 8,
        out_specs=(grid, grid, rows, rows) + (P(),) * 6,
        check_vma=False,
    )
```

```python
import functools

import jax
import jax.numpy as jnp
import numpy as np
from jax import lax
from jax.experimental import pallas as pl
from jax.experimental.pallas import tpu as pltpu
from jax.sharding import PartitionSpec as P

HEADS = 32
WIN = 8
SHIFT = 4
SIDE = 16
TOK = SIDE * SIDE
D = 1024
HALO = (SIDE - SHIFT) * SHIFT
CORNER = SHIFT * SHIFT
BORDER = 2 * HALO + CORNER
CAT = TOK + BORDER
WIN2 = WIN * WIN
WINDOWS = TOK // WIN2
GROUP = 4
GROUPS = HEADS // GROUP
LANES = 128
WIDE = GROUP * WIN2
FUSED = 8
EXTRA = 2 * LANES
AXES = ("rep", "row", "col")

norm_epsilon = 1e-05
unit_floor = 1e-12
f32 = jnp.float32
bf16 = jnp.bfloat16
VMEM_LIMIT = 56 * 1024 * 1024


def window_order():
    order = np.zeros((TOK, CAT), np.float32)
    for r in range(SIDE):
        for c in range(SIDE):
            n = ((r // WIN) * 2 + c // WIN) * WIN2 + (r % WIN) * WIN + c % WIN
            rr, cc = r + SHIFT, c + SHIFT
            if rr < SIDE and cc < SIDE:
                m = rr * SIDE + cc
            elif cc < SIDE:
                m = TOK + (rr - SIDE) * (SIDE - SHIFT) + cc - SHIFT
            elif rr < SIDE:
                m = TOK + HALO + (rr - SHIFT) * SHIFT + (cc - SIDE)
            else:
                m = TOK + 2 * HALO + (rr - SIDE) * SHIFT + (cc - SIDE)
            order[n, m] = 1.0
    return order


def border_spread():
    spread = np.zeros((TOK, BORDER), np.float32)
    for r in range(SIDE):
        for c in range(SIDE):
            if r < SHIFT and c >= SHIFT:
                spread[r * SIDE + c, r * (SIDE - SHIFT) + c - SHIFT] = 1.0
            elif r >= SHIFT and c < SHIFT:
                spread[r * SIDE + c, HALO + (r - SHIFT) * SHIFT + c] = 1.0
            elif r < SHIFT and c < SHIFT:
                spread[r * SIDE + c, 2 * HALO + r * SHIFT + c] = 1.0
    return spread


def head_mask():
    rows = np.arange(WIDE)[:, None] // WIN2
    cols = np.arange(LANES)[None, :] // (LANES // GROUP)
    return (rows == cols).astype(np.float32)


def head_sums():
    heads = np.arange(2 * LANES) // (LANES // GROUP)
    return (heads[:, None] == heads[None, :]).astype(np.float32)


def mm(a, b):
    return jnp.dot(a, b, preferred_element_type=f32)


def mm_tb(a, b):
    return lax.dot_general(a, b, (((1,), (1,)), ((), ())), preferred_element_type=f32)


def mm_ta(a, b):
    return lax.dot_general(a, b, (((0,), (0,)), ((), ())), preferred_element_type=f32)


def exact_sums(values, ones):
    high = values.astype(bf16)
    low = (values - high.astype(f32)).astype(bf16)
    return mm(high, ones) + mm(low, ones)


def stacked_heads(x, mask):
    return jnp.concatenate((x, x, x, x), axis=0) * mask


def in_step(parts):
    while parts:
        parts = [part for part in parts if next(part, parts) is not parts]


def split_border(border, n, row, col, cor):
    row[n] = border[:HALO]
    col[n] = border[HALO : 2 * HALO]
    cor[n] = border[2 * HALO :]


def pack_kernel(tok, cot, spread_t, row, col, cor):
    for n, ref in enumerate((tok, cot)):
        split_border(mm(spread_t[...], ref[...]).astype(bf16), n, row, col, cor)


def local_kernel(
    place, row_field, col_field, logit_scale, tok, cot, row_in, col_in, cor_in, order, order_t, mask_ref, ones_ref,
    wqkv_hbm, bqkv, bias_hbm, wproj_hbm, bproj, gain, shift,
    send, keep, own, row, col, cor, small,
    wqkv, wproj, bias_t, cat, qkv, att, cos, units, inverses, grad, wide, branch, pos, vec,
    x, mixed, gp_send, gp_keep, g_send, g_keep, border, sems, out_sems,
):
    loads = []

    def load(source, target):
        copy = pltpu.make_async_copy(source, target, sems.at[len(loads)])
        copy.start()
        loads.append(copy)
        return copy

    def gather(n, whole):
        first, copies = 0, []
        for source, count in ((whole, TOK), (row_in.at[n], HALO), (col_in.at[n], HALO), (cor_in.at[n], CORNER)):
            copies.append(load(source, cat.at[n, pl.ds(first, count), :]))
            first += count
        return copies

    tok_loads = gather(0, tok)
    weight_loads = [load(wqkv_hbm.at[:, pl.ds(t * D, D)], wqkv.at[:, pl.ds(t * D, D)]) for t in range(3)]
    bias_load = load(bias_hbm, bias_t)
    cot_loads = gather(1, cot)
    proj_load = load(wproj_hbm, wproj)

    p = place[2]
    half = D // 2
    stores = []

    def write(source, target):
        copy = pltpu.make_async_copy(source, target, out_sems.at[len(stores)])
        copy.start()
        stores.append(copy)

    for copy in tok_loads:
        copy.wait()
    x[...] = mm(order[...], cat[0]).astype(bf16)
    write(x, send.at[:, pl.ds(3 * half, D)])

    sub = lax.broadcasted_iota(jnp.int32, (WIN2, WIDE), 0)
    lane = lax.broadcasted_iota(jnp.int32, (WIN2, WIDE), 1) % WIN2
    row_ids, col_ids = [], []
    for i in range(SIDE):
        row_ids.append(row_field[0, lax.rem(place[0] + SHIFT + i, row_field.shape[1])] * 1024)
        col_ids.append(col_field[0, lax.rem(place[1] + SHIFT + i, col_field.shape[1])])

    def spread_ids(ids, index):
        out = jnp.zeros((WIN2, WIDE), jnp.int32)
        for i in range(WIN):
            out = jnp.where(index == i, ids[i], out)
        return out

    row_same, col_same = [], []
    for n in range(2):
        part = slice(n * WIN, (n + 1) * WIN)
        row_same.append(spread_ids(row_ids[part], sub // WIN) == spread_ids(row_ids[part], lane // WIN))
        col_same.append(spread_ids(col_ids[part], sub % WIN) == spread_ids(col_ids[part], lane % WIN))
    allowed = [(row_same[w // 2] & col_same[w % 2]).astype(f32) for w in range(WINDOWS)]
    mask = mask_ref[...]
    mask_pair = jnp.concatenate((mask, mask), axis=1)
    ones = ones_ref[...]
    wide_lane = lax.broadcasted_iota(jnp.int32, (1, WIDE), 1) // WIN2

    odd_head = lax.broadcasted_iota(jnp.int32, (WIN2, LANES), 1) // (LANES // GROUP) % 2 == 1

    def own_heads(full, dtype):
        picked = jnp.concatenate((full[:WIN2, :LANES], full[WIN2:, LANES:]), axis=0).astype(dtype).T
        return jnp.where(odd_head, picked[WIN2:], picked[:WIN2])

    head_lane = lax.broadcasted_iota(jnp.int32, (WIN2, LANES), 1) // (LANES // GROUP)

    def pick_heads(full):
        out = full[:WIN2]
        for h in range(1, GROUP):
            out = jnp.where(head_lane == h, full[h * WIN2 : (h + 1) * WIN2], out)
        return out

    window_rows = [slice(w * WIN2, (w + 1) * WIN2) for w in range(WINDOWS)]

    def scale_of(g):
        out = jnp.zeros((1, WIDE), f32)
        for h in range(GROUP):
            out = jnp.where(wide_lane == h, logit_scale[g * GROUP + h], out)
        return out

    for t in range(3):
        weight_loads[t].wait()

        @pl.loop(0, 2)
        def _(n):
            cols = pl.ds(pl.multiple_of(t * D + n * 512, 512), 512)
            qkv[:, cols] = (mm(x[...], wqkv[:, cols]) + bqkv[:, cols]).astype(bf16)

    bias_load.wait()

    def attend(g):
        at = pl.multiple_of(g * LANES, LANES)
        qs = pl.ds(at, LANES)
        v = qkv[:, pl.ds(at + 2 * D, LANES)]
        raw = jnp.concatenate((qkv[:, qs], qkv[:, pl.ds(at + D, LANES)]), axis=1).astype(f32)
        total = exact_sums(raw * raw, ones)
        yield
        inv = lax.rsqrt(jnp.maximum(total, unit_floor * unit_floor))
        unit = (raw * inv).astype(bf16)
        qu, ku = unit[:, :LANES], unit[:, LANES:]
        cosines = [mm_tb(ku[rows], stacked_heads(qu[rows], mask)) for rows in window_rows]
        yield
        sc = scale_of(g)
        bias = bias_t[g]
        attentions = []
        for w in range(WINDOWS):
            weights = jnp.exp(sc * cosines[w] + bias) * allowed[w]
            total = jnp.sum(weights, axis=0, keepdims=True)
            attentions.append((weights * (1.0 / total)).astype(bf16))
        products = [mm_ta(attentions[w], v[window_rows[w]]) for w in range(WINDOWS)]
        yield
        for n in range(2):
            inverses[n, :, qs] = inv[:, n * LANES : (n + 1) * LANES]
            units[n, :, qs] = unit[:, n * LANES : (n + 1) * LANES]
        for w in range(WINDOWS):
            att[g, w] = attentions[w]
            cos[g, w] = cosines[w]
        mixed[:, qs] = jnp.concatenate([pick_heads(product).astype(bf16) for product in products], axis=0)

    @pl.loop(0, GROUPS // FUSED)
    def _(n):
        in_step([attend(n * FUSED + u) for u in range(FUSED)])

    write(mixed, send.at[:, pl.ds(0, D)])
    proj_load.wait()
    for copy in cot_loads:
        copy.wait()
    grad[...] = mm(order[...], cat[1]).astype(bf16)

    @pl.loop(0, 4)
    def _(n):
        cols = pl.ds(pl.multiple_of(n * 256, 256), 256)
        wide[:, cols] = mm(mixed[...], wproj[:, cols]) + bproj[:, cols]

    gain_v = gain[...]
    shift_v = shift[...]

    projected = wide[...]
    centre = projected - jnp.mean(projected, axis=-1, keepdims=True)
    inv_std = lax.rsqrt(jnp.mean(centre * centre, axis=-1, keepdims=True) + norm_epsilon)
    normed = centre * inv_std
    branch[...] = (normed * gain_v + shift_v).astype(bf16)
    go = grad[...].astype(f32)
    gn = go * gain_v
    gpf = inv_std * (
        gn - jnp.mean(gn, axis=-1, keepdims=True) - normed * jnp.mean(gn * normed, axis=-1, keepdims=True)
    )
    grad[...] = gpf.astype(bf16)
    vec[:, 3 * D : 4 * D] = jnp.sum(gpf, axis=0, keepdims=True)
    vec[:, 4 * D : 5 * D] = jnp.sum(go * normed, axis=0, keepdims=True)
    vec[:, 5 * D : 6 * D] = jnp.sum(go, axis=0, keepdims=True)

    gp_keep[...] = grad[:, pl.ds(pl.multiple_of(p * half, half), half)]
    gp_send[...] = grad[:, pl.ds(pl.multiple_of((1 - p) * half, half), half)]
    write(gp_keep, keep.at[:, pl.ds(0, half)])
    write(gp_send, send.at[:, pl.ds(D, half)])

    def give_back(n, values):
        border[n] = mm(order_t[...], values).astype(bf16)
        first = 0
        for ref, count in ((own, TOK), (row, HALO), (col, HALO), (cor, CORNER)):
            write(border.at[n, pl.ds(first, count), :], ref.at[n])
            first += count

    give_back(0, branch[...])

    @pl.loop(0, 4)
    def _(n):
        cols = pl.ds(pl.multiple_of(n * 256, 256), 256)
        branch[:, cols] = mm_tb(grad[...], wproj[cols, :]).astype(bf16)

    def attend_back(g):
        at = pl.multiple_of(g * LANES, LANES)
        qs = pl.ds(at, LANES)
        v = qkv[:, pl.ds(at + 2 * D, LANES)]
        qu = units[0, :, qs]
        ku = units[1, :, qs]
        gmx = branch[:, qs]
        both = [
            stacked_heads(jnp.concatenate((gmx[rows], qu[rows]), axis=1), mask_pair) for rows in window_rows
        ]
        grad_atts = [mm_tb(v[window_rows[w]], both[w][:, :LANES]) for w in range(WINDOWS)]
        yield
        sc = scale_of(g)
        pos_sum = jnp.zeros((WIN2, WIDE), f32)
        sc_sum = jnp.zeros((WIN2, WIDE), f32)
        pairs, products = [], []
        for w in range(WINDOWS):
            attention = att[g, w]
            att_f = attention.astype(f32)
            dots = jnp.sum(grad_atts[w] * att_f, axis=0, keepdims=True)
            grad_scores = att_f * (grad_atts[w] - dots)
            pos_sum = pos_sum + grad_scores
            sc_sum = sc_sum + grad_scores * cos[g, w]
            grad_cos = (sc * grad_scores).astype(bf16)
            pairs.append(mm(jnp.concatenate((attention, grad_cos), axis=0), both[w]))
            products.append(mm_ta(ku[window_rows[w]], grad_cos))
        yield
        gqu = jnp.concatenate([own_heads(product, f32) for product in products], axis=0)
        gku = jnp.concatenate([pair[WIN2:, LANES:] for pair in pairs], axis=0)
        got = jnp.concatenate((gqu, gku), axis=1)
        inv = jnp.concatenate((inverses[0, :, qs], inverses[1, :, qs]), axis=1)
        unit = jnp.concatenate((qkv[:, qs], qkv[:, pl.ds(at + D, LANES)]), axis=1).astype(f32) * inv
        along = mm((got * unit).astype(bf16), ones)
        yield
        got = inv * (got - unit * along)
        results = [got[:, :LANES], got[:, LANES:], jnp.concatenate([pair[:WIN2, :LANES] for pair in pairs], axis=0)]
        turned = pos_sum.T
        pos_parts = []
        for h in range(GROUP):
            upper = turned[h * WIN2 : h * WIN2 + 32]
            lower = turned[h * WIN2 + 32 : (h + 1) * WIN2]
            pos_parts.append(jnp.concatenate((upper, lower), axis=1))
        pos[pl.ds(pl.multiple_of(g * LANES, LANES), LANES), :] = jnp.concatenate(pos_parts, axis=0)
        vec[:, pl.ds(pl.multiple_of(6 * D + g * WIDE, WIDE), WIDE)] = jnp.sum(sc_sum, axis=0, keepdims=True)
        for n in range(3):
            vec[:, pl.ds(at + n * D, LANES)] = jnp.sum(results[n], axis=0, keepdims=True)
        inner = pl.multiple_of(lax.rem(g, GROUPS // 2) * LANES, LANES)
        yield

        def put(ref):
            for n in range(3):
                ref[:, pl.ds(n * half + inner, LANES)] = results[n].astype(bf16)

        side = g // (GROUPS // 2)
        pl.when(side == p)(lambda: put(g_keep))
        pl.when(side != p)(lambda: put(g_send))

    @pl.loop(0, GROUPS // FUSED)
    def _(n):
        in_step([attend_back(n * FUSED + u) for u in range(FUSED)])

    write(g_keep, keep.at[:, pl.ds(half, 3 * half)])
    write(g_send, send.at[:, pl.ds(5 * half, 3 * half)])

    @pl.loop(0, 64, unroll=8)
    def _(n):
        rows = pl.ds(pl.multiple_of(n * 16, 16), 16)
        tiles = []
        for m in range(2):
            at = pl.multiple_of(lax.rem(2 * n + m, 64) * LANES, LANES)
            tiles.append(jnp.broadcast_to(vec[:, pl.ds(at, LANES)], (8, LANES)))
        small[rows, :] = jnp.concatenate((pos[rows, :], jnp.concatenate(tiles, axis=0)), axis=1).astype(bf16)

    @pl.loop(0, 4)
    def _(n):
        rows = pl.ds(pl.multiple_of(n * 256, 256), 256)
        total = jnp.zeros((TOK, 256), f32)
        for t in range(3):
            for ref, side in ((g_keep, p), (g_send, 1 - p)):
                cols = pl.ds(pl.multiple_of(t * D + side * half, half), half)
                total = total + mm_tb(ref[:, t * half : (t + 1) * half], wqkv[rows, cols])
        branch[:, rows] = total.astype(bf16)

    give_back(1, branch[...])
    for copy in stores:
        copy.wait()


def weight_grad_kernel(send, keep, other, out, own_v, other_v, keep_v, part, in_sems, out_sems):
    half = D // 2
    loads, stores = [], []

    def load(source, target, first, width):
        cols = pl.ds(first, width)
        copy = pltpu.make_async_copy(source.at[:, cols], target.at[:, cols], in_sems.at[len(loads)])
        copy.start()
        loads.append(copy)

    load(send, own_v, 3 * half, D)
    load(keep, keep_v, half, half)
    load(other, other_v, 3 * half, D)
    load(other, other_v, 5 * half, half)
    load(keep, keep_v, D, D)
    load(other, other_v, 6 * half, D)
    load(send, own_v, 0, D)
    load(other, other_v, 0, 3 * half)
    load(keep, keep_v, 0, half)

    def multiply(t, feature, grad_keep, grad_other):
        grad = jnp.concatenate(
            (keep_v[:, grad_keep : grad_keep + half], other_v[:, grad_other : grad_other + half]), axis=0
        )
        for m in range(2):
            cols = slice(feature + m * half, feature + (m + 1) * half)
            value = jnp.concatenate((own_v[:, cols], other_v[:, cols]), axis=0)
            part[t, m * half : (m + 1) * half, :] = mm_ta(value, grad).astype(bf16)
        copy = pltpu.make_async_copy(part.at[t], out.at[:, pl.ds(t * half, half)], out_sems.at[t])
        copy.start()
        stores.append(copy)

    for n in range(4):
        loads[n].wait()
    multiply(0, 3 * half, half, 5 * half)
    for n in range(4, 6):
        loads[n].wait()
    multiply(1, 3 * half, 2 * half, 6 * half)
    multiply(2, 3 * half, 3 * half, 7 * half)
    for n in range(6, 9):
        loads[n].wait()
    multiply(3, 0, 0, 2 * half)
    for copy in stores:
        copy.wait()


def last_kernel(
    got_hbm, qkv_out, proj_out, pos_out, qkv_bias, proj_bias, gain, shift, scale, got, total, small, sems
):
    half = D // 2
    pairs, _, rows, _ = got.shape
    steps = sems.shape[0]
    each = pairs // steps
    loads = []
    for n in range(steps):
        part = pl.ds(n * each, each)
        loads.append(pltpu.make_async_copy(got_hbm.at[part], got.at[part], sems.at[n]))
        loads[n].start()
    for n in range(steps):
        loads[n].wait()
        here = slice(n * each, (n + 1) * each)
        for side in range(2):
            value = jnp.sum(got[here, side, :, 0 : 4 * half].astype(f32), axis=0)
            total[side] = value if n == 0 else total[side] + value
        count = 2 * each * rows
        small[n * count : (n + 1) * count, :] = got[here, :, :, 4 * half :].astype(f32).reshape(count, EXTRA)
    for side in range(2):
        for t in range(3):
            first = t * D + side * half
            qkv_out[:, first : first + half] = total[side, :, t * half : (t + 1) * half]
        proj_out[:, side * half : (side + 1) * half] = total[side, :, 3 * half :]
    folded = small[:, 0:LANES].reshape(HEADS, WIN2 // 2, LANES)
    pos_out[:, 0 : WIN2 // 2, :] = folded[:, :, 0:WIN2]
    pos_out[:, WIN2 // 2 :, :] = folded[:, :, WIN2:]
    first = 0
    for ref in (qkv_bias, proj_bias, gain, shift):
        for n in range(ref.shape[0] // LANES):
            ref[n * LANES : (n + 1) * LANES] = small[8 * (first + n), LANES:]
        first += ref.shape[0] // LANES
    parts = small[8 * first : 8 * first + LANES, LANES:]
    lane = lax.broadcasted_iota(jnp.int32, (LANES, LANES), 1)
    at = lax.broadcasted_iota(jnp.int32, (LANES, LANES), 0)
    left = jnp.sum(parts[:, :WIN2], axis=1, keepdims=True)
    right = jnp.sum(parts[:, WIN2:], axis=1, keepdims=True)
    heads = jnp.where(at == lane // 2 * 8, jnp.where(lane % 2 == 0, left, right), 0.0)
    heads = jnp.sum(heads, axis=0, keepdims=True)
    scale[...] = heads[0, :HEADS]


def finish_kernel(tok, cot, own, row, col, cor, spread, block_out, grad_tokens):
    for n, (base, out) in enumerate(((tok, block_out), (cot, grad_tokens))):
        border = jnp.concatenate((row[n], col[n], cor[n]), axis=0)
        moved = own[n].astype(f32) + mm(spread[...], border)
        out[...] = (base[...].astype(f32) + moved).astype(bf16)


def sds(shape, dtype):
    return jax.ShapeDtypeStruct(shape, dtype)


VM = pl.BlockSpec(memory_space=pltpu.VMEM)
SM = pl.BlockSpec(memory_space=pltpu.SMEM)
ANY = pl.BlockSpec(memory_space=pl.ANY)


def call(kernel, outs, scratch=(), specs=None, flops=0, bytes_accessed=0, out_specs=None, limit=VMEM_LIMIT):
    return pl.pallas_call(
        kernel,
        out_shape=outs,
        in_specs=specs,
        out_specs=out_specs or jax.tree.map(lambda _: VM, outs),
        scratch_shapes=list(scratch),
        compiler_params=pltpu.CompilerParams(vmem_limit_bytes=limit),
        cost_estimate=pl.CostEstimate(flops=flops, bytes_accessed=bytes_accessed, transcendentals=0),
    )


def neighbour(by_row, by_col):
    rows, cols = lax.axis_size("row"), lax.axis_size("col")
    reps = lax.axis_size("rep")
    pairs = []
    for s in range(reps):
        for r in range(rows):
            for c in range(cols):
                to = (s * rows + (r + by_row) % rows) * cols + (c + by_col) % cols
                pairs.append(((s * rows + r) * cols + c, to))
    return pairs


def per_device(
    tokens, cotangent, row_field, col_field, qkv_weight, qkv_bias, logit_scale, position_bias,
    proj_weight, proj_bias, norm_gain, norm_shift,
):
    devices = lax.axis_size(AXES)
    order = jnp.asarray(window_order(), bf16)
    order_t = jnp.asarray(window_order().T, bf16)
    spread = jnp.asarray(border_spread(), bf16)
    spread_t = jnp.asarray(border_spread().T, bf16)
    mask = jnp.asarray(head_mask(), bf16)
    ones = jnp.asarray(head_sums(), bf16)
    tok = tokens[0].reshape(TOK, D)
    cot = cotangent[0].reshape(TOK, D)

    row_in, col_in, cor_in = call(
        pack_kernel, (sds((2, HALO, D), bf16), sds((2, HALO, D), bf16), sds((2, CORNER, D), bf16)), (), [VM] * 3,
        flops=10**8, bytes_accessed=2**21,
    )(tok, cot, spread_t)
    row_in = lax.ppermute(row_in, AXES, neighbour(-1, 0))
    col_in = lax.ppermute(col_in, AXES, neighbour(0, -1))
    cor_in = lax.ppermute(cor_in, AXES, neighbour(-1, -1))

    col_index = lax.axis_index("col")
    place = jnp.stack((lax.axis_index("row") * SIDE, col_index * SIDE, col_index % 2)).astype(jnp.int32)
    bias_t = position_bias.reshape(GROUPS, GROUP, WIN2, WIN2).transpose(0, 3, 1, 2).reshape(GROUPS, WIN2, WIDE)

    send, keep, own, row, col, cor, small = call(
        local_kernel,
        (
            sds((TOK, 4 * D), bf16), sds((TOK, 2 * D), bf16),
            sds((2, TOK, D), bf16), sds((2, HALO, D), bf16), sds((2, HALO, D), bf16), sds((2, CORNER, D), bf16),
            sds((D, EXTRA), bf16),
        ),
        [
            pltpu.VMEM((D, 3 * D), bf16), pltpu.VMEM((D, D), bf16), pltpu.VMEM((GROUPS, WIN2, WIDE), f32),
            pltpu.VMEM((2, CAT, D), bf16), pltpu.VMEM((TOK, 3 * D), bf16),
            pltpu.VMEM((GROUPS, WINDOWS, WIN2, WIDE), bf16), pltpu.VMEM((GROUPS, WINDOWS, WIN2, WIDE), f32),
            pltpu.VMEM((2, TOK, D), bf16), pltpu.VMEM((2, TOK, D), f32), pltpu.VMEM((TOK, D), bf16),
            pltpu.VMEM((TOK, D), f32), pltpu.VMEM((TOK, D), bf16), pltpu.VMEM((HEADS * 32, LANES), f32),
            pltpu.VMEM((1, 8 * D), f32), pltpu.VMEM((TOK, D), bf16), pltpu.VMEM((TOK, D), bf16),
            pltpu.VMEM((TOK, D // 2), bf16), pltpu.VMEM((TOK, D // 2), bf16), pltpu.VMEM((TOK, 3 * D // 2), bf16),
            pltpu.VMEM((TOK, 3 * D // 2), bf16), pltpu.VMEM((2, CAT, D), bf16),
            pltpu.SemaphoreType.DMA((13,)), pltpu.SemaphoreType.DMA((14,)),
        ],
        [SM] * 4 + [ANY] * 5 + [VM] * 4 + [ANY, VM, ANY, ANY, VM, VM, VM],
        flops=5 * 10**9, bytes_accessed=20 * 2**20, out_specs=(ANY,) * 6 + (VM,),
    )(
        place, row_field, col_field, logit_scale, tok, cot, row_in, col_in, cor_in, order, order_t, mask, ones,
        qkv_weight, qkv_bias.reshape(1, -1), bias_t, proj_weight, proj_bias.reshape(1, -1),
        norm_gain.reshape(1, -1), norm_shift.reshape(1, -1),
    )
    cores = [(i, i ^ 1) for i in range(lax.axis_size("col"))]
    other = lax.ppermute(send, "col", cores)
    rows = D // devices
    small = lax.all_to_all(small.reshape(devices, rows, EXTRA), AXES, 0, 0, tiled=True)
    row = lax.ppermute(row, AXES, neighbour(1, 0))
    col = lax.ppermute(col, AXES, neighbour(0, 1))
    cor = lax.ppermute(cor, AXES, neighbour(1, 1))
    part = call(
        weight_grad_kernel,
        sds((D, 2 * D + EXTRA), bf16),
        [
            pltpu.VMEM((TOK, 4 * D), bf16), pltpu.VMEM((TOK, 4 * D), bf16), pltpu.VMEM((TOK, 2 * D), bf16),
            pltpu.VMEM((4, D, D // 2), bf16), pltpu.SemaphoreType.DMA((9,)), pltpu.SemaphoreType.DMA((4,)),
        ],
        [ANY] * 3,
        flops=8 * TOK * D * D, bytes_accessed=9 * 2**20, out_specs=ANY,
    )(send, keep, other)
    part, small = lax.optimization_barrier((part.reshape(devices, rows, -1), small))
    small = jnp.sum(small.astype(f32), axis=0).astype(bf16)
    part = part.at[:, :, 2 * D :].set(jnp.broadcast_to(small[None], (devices, rows, EXTRA)))
    got = lax.all_to_all(part, AXES, 0, 0, tiled=True)
    block_out, grad_tokens = call(
        finish_kernel, (sds((TOK, D), bf16), sds((TOK, D), bf16)), (), [VM] * 7, flops=10**8, bytes_accessed=2**22, limit=20 * 2**20
    )(tok, cot, own, row, col, cor, spread)
    outs = (
        sds((rows, 3 * D), f32), sds((rows, D), f32), sds((HEADS, WIN2, WIN2), f32), sds((3 * D,), f32), sds((D,), f32),
        sds((D,), f32), sds((D,), f32), sds((HEADS,), f32),
    )
    got = got.reshape(devices // 2, 2, rows, 2 * D + EXTRA)
    steps = min(4, devices // 2)
    grad_qkv_weight, grad_proj_weight, grad_position, g_qkv_bias, g_proj_bias, g_gain, g_shift, g_scale = call(
        last_kernel,
        outs,
        [
            pltpu.VMEM(got.shape, bf16), pltpu.VMEM((2, rows, 2 * D), f32), pltpu.VMEM((D, EXTRA), f32),
            pltpu.SemaphoreType.DMA((steps,)),
        ],
        [ANY],
        flops=10**7, bytes_accessed=2**22,
    )(got)
    return (
        block_out.reshape(1, SIDE, SIDE, D), grad_tokens.reshape(1, SIDE, SIDE, D), grad_qkv_weight, grad_proj_weight, g_qkv_bias, g_proj_bias,
        g_gain, g_shift, g_scale, grad_position,
    )


def solution(mesh):
    grid = P("rep", "row", "col", None)
    rows = P(AXES, None)
    return jax.shard_map(
        per_device,
        mesh=mesh,
        in_specs=(grid, grid, P("rep", None), P("rep", None)) + (P(),) * 8,
        out_specs=(grid, grid, rows, rows) + (P(),) * 6,
        check_vma=False,
    )
```
